32 devices in a mesh: cell: 16 (over z, y, core), brick: 2 (over x).
Axes of the slice: x: 2, y: 2, z: 4, core: 2. Of those that a mesh axis runs over, the one named last changes fastest.
Arguments:
- features: bfloat16 [16, 2, 128, 256], P('cell', 'brick'), may hold values from -6 to 6
- species: int32 [16, 2, 128], P('cell', 'brick'), may hold values from 0 to 3
- species_table: bfloat16 [4, 256], replicated, may hold values from -3 to 3
- neighbours: int32 [16, 2, 64, 128], P('cell', 'brick'), may hold values from 0 to 191
- counts: int32 [16, 2, 128], P('cell', 'brick'), may hold values from 1 to 64
- send_lists: int32 [16, 2, 2, 32], P('cell', 'brick'), may hold values from 0 to 127
- distances: float32 [16, 2, 64, 128], P('cell', 'brick'), may hold values from 0.05 to 1
- head_decay: float32 [8], replicated, may hold values from 0.25 to 4
- norm_gain: float32 [256], replicated, may hold values from 0.5 to 1.5
- readout: float32 [256], replicated, may hold values from -0.375 to 0.375
- targets: float32 [16, 2, 128], P('cell', 'brick'), may hold values from -6 to 6
- master: float32 [4, 256, 256], P(None, 'cell'), as said below
- moment: float32 [4, 256, 256], P(None, 'cell'), may hold values from -3 to 3
- second: float32 [4, 256, 256], P(None, 'cell'), may hold values from 0.1 to 1
Outputs:
- energies: float32 [16, 2, 128], P('cell', 'brick')
- moment_new: float32 [4, 256, 256], P(None, 'cell')
- second_new: float32 [4, 256, 256], P(None, 'cell')
- adam_step: float32 [4, 256, 256], P(None, 'cell')
The draws below stay inside these ranges and needn't reach their ends.
Inputs may be any that keep to these rules, and one draw needn't show every extreme that they name: `master`: projection entries lie within -48 * 256^-0.5 and 48 * 256^-0.5.
All inputs are finite; a program needn't handle non-finite values.
Results may differ from the reference program's by a relative error of at most 0.0045.
The reference program's roundings to bfloat16 on the way count: a program that leaves them out, or rounds other values in their place, can miss the bound.
Values may be sent and summed in bfloat16 or wider, within the bound.
No kernel may reach another device: no remote copies, remote signals or barrier semaphores. Data moves between devices by JAX's collectives and lax.ppermute only.
A program may use at most 64 MiB of HBM per device.

```python
import math
import jax
import jax.numpy as jnp
from jax import lax

C = 256
HEADS = 8
K = 64
TILE = 128
SPECIES = 4
ATOMS_DEV = 128
GHOST_SLOT = 32
CELLS = 16
BRICK_COUNT = 2
TABLE = 192


def draw_master(key, part):
    base_draw = jax.random.normal(key, (4, C, C), jnp.float32)
    base_draw = jnp.clip(base_draw, -6.0, 6.0) * (1.0 / math.sqrt(C))
    return base_draw


def with_ends(array, key, smallest, top_value):
    place = [jax.random.randint(jax.random.fold_in(key, axis), (), 0, length) for axis, length in enumerate(array.shape)]
    widest = array.shape.index(max(array.shape))
    next_to = place[:widest] + [(place[widest] + 1) % array.shape[widest]] + place[widest + 1:]
    return array.at[tuple(place)].set(smallest).at[tuple(next_to)].set(top_value)


def block_levels(stream_key, extent, split, smallest, high):
    loudness = 1.0
    for axis_at, shards_of in split:
        draws = jax.random.uniform(jax.random.fold_in(jax.random.fold_in(stream_key, 6), axis_at), (shards_of,), jnp.float32, smallest / len(split), high / len(split))
        loudness = loudness * jnp.repeat(jnp.exp(draws), extent[axis_at] // shards_of).reshape((-1,) + (1,) * (len(extent) - 1 - axis_at))
    return loudness


def centred(rng, extent, width, most, shards=(), kind=jnp.bfloat16):
    result = jax.random.normal(rng, extent, jnp.float32) * width
    if len(shards) > 0:
        result = block_levels(rng, extent, shards, -0.22, 0.18) * result
    return jnp.clip(result, min=-most, max=most).astype(kind)


def setup_inputs(seed: int = 0) -> dict:
    splits = jax.random.split(jax.random.key(seed), 15)
    features = centred(splits[0], (CELLS, BRICK_COUNT, ATOMS_DEV, C), 1.0, 6.0, ((0, 16), (1, 2)))
    species = with_ends(jax.random.randint(splits[1], (CELLS, BRICK_COUNT, ATOMS_DEV), 0, SPECIES), jax.random.fold_in(splits[1], 1), 0, SPECIES - 1).astype(jnp.int32)
    species_table = centred(splits[2], (SPECIES, C), 0.5, 3.0)
    neighbours = with_ends(jax.random.randint(splits[3], (CELLS, BRICK_COUNT, K, ATOMS_DEV), 0, TABLE), jax.random.fold_in(splits[3], 1), 0, TABLE - 1).astype(jnp.int32)
    counts = with_ends(jax.random.randint(splits[4], (CELLS, BRICK_COUNT, ATOMS_DEV), 1, K + 1), jax.random.fold_in(splits[4], 1), 1, K).astype(jnp.int32)
    send_lists = with_ends(jax.random.randint(splits[5], (CELLS, BRICK_COUNT, BRICK_COUNT, GHOST_SLOT), 0, ATOMS_DEV), jax.random.fold_in(splits[5], 1), 0, ATOMS_DEV - 1).astype(jnp.int32)
    distances = jnp.clip(0.05 + 0.95 * jax.random.uniform(splits[6], (CELLS, BRICK_COUNT, K, ATOMS_DEV), jnp.float32) ** block_levels(splits[6], (CELLS, BRICK_COUNT, K, ATOMS_DEV), ((0, 16), (1, 2)), -0.2, 0.2), 0.05, 1.0)
    head_decay = jnp.clip(jnp.exp(jax.random.uniform(splits[7], (HEADS,), jnp.float32, math.log(0.25), math.log(4.0))), 0.25, 4.0)
    norm_gain = jnp.clip(1.0 + 0.1 * jax.random.normal(splits[8], (C,), jnp.float32), 0.5, 1.5)
    readout = centred(splits[9], (C,), 0.0625, 0.375, (), jnp.float32)
    targets = centred(splits[10], (CELLS, BRICK_COUNT, ATOMS_DEV), 1.0, 6.0, ((0, 16), (1, 2)), jnp.float32)
    master = draw_master(jax.random.fold_in(splits[14], 71), 0)
    moment = centred(splits[12], (4, C, C), 0.5, 3.0, ((1, 16),), jnp.float32)
    second = jnp.clip(jnp.exp(math.log(1.0) - 2.3025851 * jax.random.uniform(splits[13], (4, C, C), jnp.float32) ** block_levels(splits[13], (4, C, C), ((1, 16),), -0.2, 0.2)), 0.1, 1.0)
    return dict(features=features, species=species, species_table=species_table, neighbours=neighbours, counts=counts, send_lists=send_lists, distances=distances, head_decay=head_decay, norm_gain=norm_gain, readout=readout, targets=targets, master=master, moment=moment, second=second)


loss_weight = 0.0625
epsilon_norm = 1e-06

def silu_slope(inputs):
    sigmoid_val = jax.nn.sigmoid(inputs)
    return sigmoid_val * (1.0 + inputs * (1.0 - sigmoid_val))

def normalize(embedded, norm_gain):
    rms_scale = lax.rsqrt(lax.optimization_barrier(jnp.mean(embedded * embedded, axis=-1, keepdims=True)) + epsilon_norm)
    return (embedded * rms_scale * norm_gain).astype(jnp.bfloat16)

def brick_sweep(query, key_table, value_table, embedded, neighbour_rows, local_count, local_dist, local_target, out_proj, head_decay, readout):
    atom_count, model_width = query.shape
    head_count = head_decay.shape[0]
    head_size = model_width // head_count
    slot_count = neighbour_rows.shape[0]
    score_scale = 1.0 / math.sqrt(head_size)
    table_rows = key_table.shape[0]

    def tile_step(grad_carry, tile_index):
        key_grads, value_grads = grad_carry
        row_start = (tile_index * TILE).astype(jnp.int32)
        query_tile = lax.dynamic_slice_in_dim(query, row_start, TILE, 0)
        nbr_tile = lax.dynamic_slice_in_dim(neighbour_rows, row_start, TILE, 1)
        count_tile = lax.dynamic_slice_in_dim(local_count, row_start, TILE, 0)
        dist_tile = lax.dynamic_slice_in_dim(local_dist, row_start, TILE, 1)
        embed_tile = lax.dynamic_slice_in_dim(embedded, row_start, TILE, 0)
        target_tile = lax.dynamic_slice_in_dim(local_target, row_start, TILE, 0)
        key_rows = key_table[nbr_tile].reshape(slot_count, TILE, head_count, head_size)
        value_rows = value_table[nbr_tile].reshape(slot_count, TILE, head_count, head_size)
        query_heads = query_tile.reshape(TILE, head_count, head_size)
        is_valid = (jnp.arange(slot_count)[:, None] < count_tile[None, :])[:, :, None]
        score = jnp.einsum('ahd,kahd->kah', query_heads.astype(jnp.float32), key_rows.astype(jnp.float32)) * score_scale
        score = score - head_decay[None, None, :] * dist_tile[:, :, None]
        score = jnp.where(is_valid, score, -1e+30)
        row_max = lax.optimization_barrier(jnp.max(score, axis=0, keepdims=True))
        exp_terms = jnp.where(is_valid, jnp.exp(score - row_max), 0.0)
        attention = exp_terms / lax.optimization_barrier(jnp.sum(exp_terms, axis=0, keepdims=True))
        attention_half = attention.astype(jnp.bfloat16)
        attended = jnp.einsum('kah,kahd->ahd', attention_half.astype(jnp.float32), value_rows.astype(jnp.float32))
        attended = attended.astype(jnp.bfloat16).reshape(TILE, model_width)
        updated = embed_tile + jnp.dot(attended, out_proj, preferred_element_type=jnp.float32)
        energy = lax.optimization_barrier(jnp.sum(readout * jax.nn.silu(updated), axis=-1))
        grad_energy = loss_weight * (energy - target_tile)
        grad_updated = (grad_energy[:, None] * readout * silu_slope(updated)).astype(jnp.bfloat16)
        grad_attended = jnp.dot(grad_updated, out_proj.T, preferred_element_type=jnp.float32).astype(jnp.bfloat16)
        grad_att_heads = grad_attended.reshape(TILE, head_count, head_size)
        grad_weights = jnp.einsum('ahd,kahd->kah', grad_att_heads.astype(jnp.float32), value_rows.astype(jnp.float32))
        grad_score = attention * (grad_weights - lax.optimization_barrier(jnp.sum(attention * grad_weights, axis=0, keepdims=True)))
        grad_score = grad_score.astype(jnp.bfloat16)
        grad_query = jnp.einsum('kah,kahd->ahd', grad_score.astype(jnp.float32), key_rows.astype(jnp.float32)) * score_scale
        grad_query = grad_query.astype(jnp.bfloat16).reshape(TILE, model_width)
        key_edge = grad_score.astype(jnp.float32)[..., None] * query_heads.astype(jnp.float32)[None] * score_scale
        value_edge = attention_half.astype(jnp.float32)[..., None] * grad_att_heads.astype(jnp.float32)[None]
        flattened_rows = nbr_tile.reshape(-1)
        key_grads = key_grads.at[flattened_rows].add(key_edge.reshape(-1, model_width))
        value_grads = value_grads.at[flattened_rows].add(value_edge.reshape(-1, model_width))
        return ((key_grads, value_grads), (energy, attended, grad_updated, grad_query))
    start_grads = (jnp.zeros((table_rows, model_width), jnp.float32), jnp.zeros((table_rows, model_width), jnp.float32))
    (key_grads, value_grads), stacked = lax.scan(tile_step, start_grads, jnp.arange(atom_count // TILE).astype(jnp.int32))
    energy, attended, grad_updated, grad_query = stacked
    return (key_grads, value_grads, energy.reshape(atom_count), attended.reshape(atom_count, model_width), grad_updated.reshape(atom_count, model_width), grad_query.reshape(atom_count, model_width))

def partial_owner(owner_sum, table_grads):

    def applied(peer):
        return owner_sum(table_grads, peer)
    return applied

def reference(features, species, species_table, neighbours, counts, send_lists, distances, head_decay, norm_gain, readout, targets, master, moment, second):
    attention_weights = master.astype(jnp.bfloat16)
    bricks = features.shape[1]
    atom_count = features.shape[2]
    model_width = features.shape[3]
    ghost_position = send_lists.shape[-1]

    def per_cell(grad_total, cell_inputs):
        cell_feat, cell_species, cell_nbr, cell_count, cell_send, cell_dist, cell_target = cell_inputs
        embedded = cell_feat.astype(jnp.float32) + species_table[cell_species].astype(jnp.float32)
        normed_features = normalize(embedded, norm_gain)
        flat_norm = normed_features.reshape(-1, model_width)
        query = jnp.dot(flat_norm, attention_weights[0], preferred_element_type=jnp.float32).astype(jnp.bfloat16).reshape(bricks, atom_count, model_width)
        key_all = jnp.dot(flat_norm, attention_weights[1], preferred_element_type=jnp.float32).astype(jnp.bfloat16).reshape(bricks, atom_count, model_width)
        value_all = jnp.dot(flat_norm, attention_weights[2], preferred_element_type=jnp.float32).astype(jnp.bfloat16).reshape(bricks, atom_count, model_width)

        def build_table(source_rows, brick_index):
            ghost_rows = source_rows[jnp.arange(bricks)[:, None], cell_send[:, brick_index, :]]
            return jnp.concatenate([source_rows[brick_index], ghost_rows.reshape(-1, model_width)], axis=0)

        def one_brick(brick_index):
            return brick_sweep(query[brick_index], build_table(key_all, brick_index), build_table(value_all, brick_index), embedded[brick_index], cell_nbr[brick_index], cell_count[brick_index], cell_dist[brick_index], cell_target[brick_index], attention_weights[3], head_decay, readout)
        key_grads, value_grads, energy, attended, grad_updated, grad_query = lax.map(one_brick, jnp.arange(bricks))

        def owner_sum(table_grads, peer):
            local_portion = table_grads[peer, :atom_count]
            ghost_part = table_grads[:, atom_count:].reshape(bricks, bricks, ghost_position, model_width)[:, peer]
            return local_portion.at[cell_send[peer].reshape(-1)].add(ghost_part.reshape(-1, model_width))
        grad_key = jax.vmap(partial_owner(owner_sum, key_grads))(jnp.arange(bricks)).astype(jnp.bfloat16)
        grad_value = jax.vmap(partial_owner(owner_sum, value_grads))(jnp.arange(bricks)).astype(jnp.bfloat16)
        norm_f = normed_features.astype(jnp.float32)
        grad_q = jnp.einsum('bac,bad->cd', norm_f, grad_query.astype(jnp.float32))
        key_gradient = jnp.einsum('bac,bad->cd', norm_f, grad_key.astype(jnp.float32))
        grad_v = jnp.einsum('bac,bad->cd', norm_f, grad_value.astype(jnp.float32))
        grad_o = jnp.einsum('bac,bad->cd', attended.astype(jnp.float32), grad_updated.astype(jnp.float32))
        return (grad_total + jnp.stack([grad_q, key_gradient, grad_v, grad_o]), energy)
    start_total = jnp.zeros((4, model_width, model_width), jnp.float32)
    grads, energies = lax.scan(per_cell, start_total, (features, species, neighbours, counts, send_lists, distances, targets))
    moment_new = 0.9 * moment + 0.1 * grads
    second_new = 0.999 * second + 0.001 * grads * grads
    adam_step = moment_new / (jnp.sqrt(second_new) + 1e-08)
    return (energies, moment_new, second_new, adam_step)
```

```python
import functools
import math

import jax
import jax.numpy as jnp
from jax import lax
from jax.experimental import pallas as pl
from jax.experimental.pallas import tpu as pltpu
from jax.sharding import PartitionSpec as P

LANES = 128
FAR = 1e30

loss_weight = 0.0625
epsilon_norm = 1e-06

F32 = jnp.float32
BF16 = jnp.bfloat16
NT = (((1,), (1,)), ((), ()))
TN = (((0,), (0,)), ((), ()))


def dot(a, b):
    return jnp.dot(a, b, preferred_element_type=F32)


def dot_nt(a, b):
    return lax.dot_general(a, b, NT, preferred_element_type=F32)


def dot_tn(a, b):
    return lax.dot_general(a, b, TN, preferred_element_type=F32)


def lane_gather(table, index):
    return jnp.take_along_axis(table, index, axis=1, mode="promise_in_bounds")


def to_column(row):
    n = row.shape[1]
    eye = lax.broadcasted_iota(jnp.int32, (n, n), 0) == lax.broadcasted_iota(jnp.int32, (n, n), 1)
    return jnp.sum(jnp.where(eye, row, jnp.zeros_like(row)), axis=1, keepdims=True)


def to_row(column):
    n = column.shape[0]
    eye = lax.broadcasted_iota(jnp.int32, (n, n), 0) == lax.broadcasted_iota(jnp.int32, (n, n), 1)
    return jnp.sum(jnp.where(eye, column, jnp.zeros_like(column)), axis=0, keepdims=True)


def embed_kernel(features, species, species_table, norm_gain, send_rows, embedded, normed, parcel):
    atoms = features.shape[0]
    kinds = species_table.shape[0]
    column = to_column(species[...])
    total = features[...].astype(F32)
    picked = jnp.zeros_like(total)
    for kind in range(kinds):
        row = species_table[kind : kind + 1, :].astype(F32)
        picked = jnp.where(column == kind, row, picked)
    total = total + picked
    embedded[...] = total
    scale = lax.rsqrt(jnp.mean(total * total, axis=-1, keepdims=True) + epsilon_norm)
    norm = (total * scale * norm_gain[...]).astype(BF16)
    normed[...] = norm
    bricks, slots = send_rows.shape
    for brick in range(bricks):
        chosen = send_rows[brick : brick + 1, :]
        picks = (lax.broadcasted_iota(jnp.int32, (atoms, slots), 0) == chosen).astype(F32).astype(BF16)
        parcel[brick] = dot_tn(picks, norm).astype(BF16)


def index_kernel(neighbours, counts, distances, rows, far, pointers, inverse, rounds):
    slots, atoms = neighbours.shape
    none = LANES - 1
    blocks = inverse.shape[0]
    slot = lax.broadcasted_iota(jnp.int32, (slots, atoms), 0)
    valid = slot < counts[...]
    own = neighbours[...]
    held = jnp.where(valid, own, -1 - slot)
    back = jnp.full((slots, atoms), none, jnp.int32)
    table_row = lax.broadcasted_iota(jnp.int32, (blocks * LANES, atoms), 0)
    last = jnp.full((blocks * LANES, atoms), none, jnp.int32)
    for j in range(slots):
        row = held[j : j + 1, :]
        back = jnp.where((held == row) & (slot > j), j, back)
        last = jnp.where(table_row == row, j, last)

    def turned(array, fill):
        padded = jnp.concatenate([array, jnp.full((LANES - slots, atoms), fill, array.dtype)], axis=0)
        return padded.T

    rows[...] = turned(own, 0)
    far[...] = turned(jnp.where(valid, distances[...], FAR), FAR)
    pointer = turned(back, none)
    steps = jnp.int32(0)
    for k in range(pointers.shape[0]):
        pointers[k] = pointer
        steps += (jnp.min(pointer) < none).astype(jnp.int32)
        if k + 1 < pointers.shape[0]:
            pointer = lane_gather(pointer, pointer)
    rounds[0] = steps
    for block in range(blocks):
        inverse[block] = last[block * LANES : (block + 1) * LANES].T


def gathered(dense, index, blocks, rows):
    result = lane_gather(dense[:, :LANES], index)
    for block in range(1, blocks):
        part = lane_gather(dense[:, block * LANES : (block + 1) * LANES], index)
        result = jnp.where(rows >= block * LANES, part, result)
    return result


def sweep_kernel(
    rounds,
    decay,
    weights,
    normed,
    ghosts,
    embedded,
    rows,
    far,
    pointers,
    inverse,
    readout,
    targets,
    energies,
    grads,
    slot_ref,
    att_ref,
    dense_ref,
    score_ref,
    *,
    table_rows,
):
    atoms, width = normed.shape
    heads = decay.shape[0]
    head_size = width // heads
    blocks = inverse.shape[0]
    padded = blocks * LANES
    scale = 1.0 / math.sqrt(head_size)
    head_of = lax.broadcasted_iota(jnp.int32, (atoms, width), 1) // head_size

    def stacked(array):
        zero = jnp.zeros_like(array)
        return jnp.concatenate([jnp.where(head_of == h, array, zero) for h in range(heads)], axis=0)

    def own_lanes(wide):
        result = wide[:atoms]
        for h in range(1, heads):
            result = jnp.where(head_of == h, wide[h * atoms : (h + 1) * atoms], result)
        return result

    def merge_duplicates():
        def step(k, carry):
            pointer = pointers[k]
            for h in range(heads):
                part = slot_ref[pl.ds(h * atoms, atoms), :]
                slot_ref[pl.ds(h * atoms, atoms), :] = part + lane_gather(part, pointer)
            return carry

        lax.fori_loop(0, rounds[0], step, 0)

    def to_table():
        for h in range(heads):
            part = slot_ref[pl.ds(h * atoms, atoms), :]
            for block in range(blocks):
                value = lane_gather(part, inverse[block])
                high = value.astype(BF16)
                at = (pl.ds(h * atoms, atoms), pl.ds(block * LANES, LANES))
                dense_ref[0, at[0], at[1]] = high
                dense_ref[1, at[0], at[1]] = (value - high.astype(F32)).astype(BF16)
        return dense_ref[0], dense_ref[1]

    norm = normed[...]
    pieces = [norm, ghosts[...]]
    if padded > table_rows:
        pieces.append(jnp.zeros((padded - table_rows, width), BF16))
    table = jnp.concatenate(pieces, axis=0)
    query = dot(norm, weights[0]).astype(BF16)
    keys = dot(table, weights[1]).astype(BF16)
    values = dot(table, weights[2]).astype(BF16)

    row_ids = rows[...]
    index = jnp.bitwise_and(row_ids, LANES - 1)
    away = far[...]
    query_stack = stacked(query)
    score_ref[...] = dot_nt(query_stack, keys)
    for h in range(heads):
        at = pl.ds(h * atoms, atoms)
        score = gathered(score_ref[at, :], index, blocks, row_ids) * scale - decay[h] * away
        terms = jnp.exp(score - jnp.max(score, axis=1, keepdims=True))
        attention = terms / jnp.sum(terms, axis=1, keepdims=True)
        att_ref[at, :] = attention
        slot_ref[at, :] = attention.astype(BF16).astype(F32)
    merge_duplicates()
    high, low = to_table()
    attended = own_lanes(dot(high, values) + dot(low, values)).astype(BF16)

    out_proj = weights[3]
    updated = embedded[...] + dot(attended, out_proj)
    sigmoid = 1.0 / (1.0 + jnp.exp(-updated))
    energy = jnp.sum(readout[...] * (updated * sigmoid), axis=1, keepdims=True)
    energies[...] = to_row(energy)
    grad_energy = loss_weight * (energy - to_column(targets[...]))
    slope = sigmoid * (1.0 + updated * (1.0 - sigmoid))
    grad_updated = (grad_energy * readout[...] * slope).astype(BF16)
    grads[3] = dot_tn(attended, grad_updated)
    grad_attended = dot_nt(grad_updated, out_proj).astype(BF16)

    attended_stack = stacked(grad_attended)
    value_grads = dot_tn(high, attended_stack) + dot_tn(low, attended_stack)
    grads[2] = dot_tn(table, value_grads.astype(BF16))
    score_ref[...] = dot_nt(attended_stack, values)
    for h in range(heads):
        at = pl.ds(h * atoms, atoms)
        grad_weights = gathered(score_ref[at, :], index, blocks, row_ids)
        attention = att_ref[at, :]
        mean = jnp.sum(attention * grad_weights, axis=1, keepdims=True)
        slot_ref[at, :] = (attention * (grad_weights - mean)).astype(BF16).astype(F32)
    merge_duplicates()
    high, low = to_table()
    grad_query = own_lanes(dot(high, keys) + dot(low, keys)) * scale
    grads[0] = dot_tn(norm, grad_query.astype(BF16))
    key_grads = (dot_tn(high, query_stack) + dot_tn(low, query_stack)) * scale
    grads[1] = dot_tn(table, key_grads.astype(BF16))


def vmem(count):
    return [pl.BlockSpec(memory_space=pltpu.VMEM)] * count


SMEM = pl.BlockSpec(memory_space=pltpu.SMEM)


def struct(shape, dtype):
    return jax.ShapeDtypeStruct(shape, dtype)


def flips(size, offset):
    return [(i, i ^ offset) for i in range(size)]


def halvings(size):
    offsets = []
    offset = size // 2
    while offset:
        offsets.append(offset)
        offset //= 2
    return offsets


def gather_cells(shard, cells):
    place = lax.axis_index("cell")
    offsets = halvings(cells)
    held = shard[None]
    for offset in offsets:
        other = lax.ppermute(held, "cell", flips(cells, offset))
        first = (place // offset) % 2 == 0
        held = jnp.where(first, jnp.concatenate([held, other]), jnp.concatenate([other, held]))
    bits = len(offsets)
    matrices, rows, width = shard.shape
    held = held.reshape((2,) * bits + shard.shape)
    held = held.transpose((bits,) + tuple(reversed(range(bits))) + (bits + 1, bits + 2))
    return held.reshape(matrices, cells * rows, width)


def reduce_cells(parts, cells):
    place = lax.axis_index("cell")
    tail = parts.shape[1:]
    for offset in reversed(halvings(cells)):
        bit = (place // offset) % 2
        pairs = parts.reshape((-1, 2) + tail)
        keep = lax.dynamic_index_in_dim(pairs, bit, 1, False)
        send = lax.dynamic_index_in_dim(pairs, 1 - bit, 1, False)
        parts = keep + lax.ppermute(send.astype(BF16), "cell", flips(cells, offset)).astype(F32)
    return parts[0]


def reduce_bricks(total, bricks):
    for offset in halvings(bricks):
        mine = total.astype(BF16)
        total = mine.astype(F32) + lax.ppermute(mine, "brick", flips(bricks, offset)).astype(F32)
    return total


def body(
    cells,
    bricks,
    features,
    species,
    species_table,
    neighbours,
    counts,
    send_lists,
    distances,
    head_decay,
    norm_gain,
    readout,
    targets,
    master,
    moment,
    second,
):
    atoms, width = features.shape[2:]
    slots = neighbours.shape[2]
    ghost_slots = send_lists.shape[3]
    heads = head_decay.shape[0]
    table_rows = atoms + bricks * ghost_slots
    blocks = -(-table_rows // LANES)
    levels = max(1, math.ceil(math.log2(slots)))

    weights = gather_cells(master.astype(BF16), cells)

    embedded, normed, parcel = pl.pallas_call(
        embed_kernel,
        out_shape=(
            struct((atoms, width), F32),
            struct((atoms, width), BF16),
            struct((bricks, ghost_slots, width), BF16),
        ),
        in_specs=vmem(5),
        out_specs=tuple(vmem(3)),
        name="embed",
    )(features[0, 0], species[0], species_table, norm_gain[None], send_lists[0, 0])

    brick = lax.axis_index("brick")
    ghosts = parcel
    for offset in range(1, bricks):
        peer = brick ^ offset
        sent = lax.dynamic_index_in_dim(parcel, peer, 0, True)
        arrived = lax.ppermute(sent, "brick", flips(bricks, offset))
        ghosts = lax.dynamic_update_slice_in_dim(ghosts, arrived, peer, 0)
    ghosts = ghosts.reshape(bricks * ghost_slots, width)

    rows, far, pointers, inverse, rounds = pl.pallas_call(
        index_kernel,
        out_shape=(
            struct((atoms, LANES), jnp.int32),
            struct((atoms, LANES), F32),
            struct((levels, atoms, LANES), jnp.int32),
            struct((blocks, atoms, LANES), jnp.int32),
            struct((1,), jnp.int32),
        ),
        in_specs=vmem(3),
        out_specs=tuple(vmem(4)) + (SMEM,),
        name="index",
    )(neighbours[0, 0], counts[0], distances[0, 0])

    energies, grads = pl.pallas_call(
        functools.partial(sweep_kernel, table_rows=table_rows),
        out_shape=(struct((1, atoms), F32), struct((4, width, width), F32)),
        in_specs=[SMEM, SMEM] + vmem(10),
        out_specs=tuple(vmem(2)),
        scratch_shapes=[
            pltpu.VMEM((heads * atoms, LANES), F32),
            pltpu.VMEM((heads * atoms, LANES), F32),
            pltpu.VMEM((2, heads * atoms, blocks * LANES), BF16),
            pltpu.VMEM((heads * atoms, blocks * LANES), F32),
        ],
        compiler_params=pltpu.CompilerParams(vmem_limit_bytes=32 * 1024 * 1024),
        name="sweep",
    )(
        rounds,
        head_decay,
        weights,
        normed,
        ghosts,
        embedded,
        rows,
        far,
        pointers,
        inverse,
        readout[None],
        targets[0],
    )

    parts = grads.reshape(4, cells, width // cells, width).transpose(1, 0, 2, 3)
    owned = reduce_bricks(reduce_cells(parts, cells), bricks)
    moment_new = 0.9 * moment + 0.1 * owned
    second_new = 0.999 * second + 0.001 * owned * owned
    adam_step = moment_new / (jnp.sqrt(second_new) + 1e-08)
    return (energies[None], moment_new, second_new, adam_step)


def solution(mesh):
    return jax.shard_map(
        functools.partial(body, mesh.shape["cell"], mesh.shape["brick"]),
        mesh=mesh,
        in_specs=(
            P("cell", "brick", None, None),
            P("cell", "brick", None),
            P(),
            P("cell", "brick", None, None),
            P("cell", "brick", None),
            P("cell", "brick", None, None),
            P("cell", "brick", None, None),
            P(),
            P(),
            P(),
            P("cell", "brick", None),
            P(None, "cell", None),
            P(None, "cell", None),
            P(None, "cell", None),
        ),
        out_specs=(
            P("cell", "brick", None),
            P(None, "cell", None),
            P(None, "cell", None),
            P(None, "cell", None),
        ),
        check_vma=False,
    )
```

```python
import functools
import math

import jax
import jax.numpy as jnp
from jax import lax
from jax.experimental import pallas as pl
from jax.experimental.pallas import tpu as pltpu
from jax.sharding import PartitionSpec as P

CHUNK = 64
FAR = 1e30

loss_weight = 0.0625
epsilon_norm = 1e-06

F32 = jnp.float32
BF16 = jnp.bfloat16
NT = (((1,), (1,)), ((), ()))
TN = (((0,), (0,)), ((), ()))


def dot(a, b):
    return jnp.dot(a, b, preferred_element_type=F32)


def dot_nt(a, b):
    return lax.dot_general(a, b, NT, preferred_element_type=F32)


def dot_tn(a, b):
    return lax.dot_general(a, b, TN, preferred_element_type=F32)


def to_column(row):
    n = row.shape[1]
    eye = lax.broadcasted_iota(jnp.int32, (n, n), 0) == lax.broadcasted_iota(jnp.int32, (n, n), 1)
    return jnp.sum(jnp.where(eye, row, jnp.zeros_like(row)), axis=1, keepdims=True)


def to_row(column):
    n = column.shape[0]
    eye = lax.broadcasted_iota(jnp.int32, (n, n), 0) == lax.broadcasted_iota(jnp.int32, (n, n), 1)
    return jnp.sum(jnp.where(eye, column, jnp.zeros_like(column)), axis=0, keepdims=True)


def embed_kernel(features, species, species_table, norm_gain, send_rows, embedded, normed, normed_t, parcel):
    atoms = features.shape[0]
    kinds = species_table.shape[0]
    column = to_column(species[...])
    total = features[...].astype(F32)
    picked = jnp.zeros_like(total)
    for kind in range(kinds):
        row = species_table[kind : kind + 1, :].astype(F32)
        picked = jnp.where(column == kind, row, picked)
    total = total + picked
    embedded[...] = total
    scale = lax.rsqrt(jnp.mean(total * total, axis=-1, keepdims=True) + epsilon_norm)
    norm = total * scale * norm_gain[...]
    half = norm.astype(BF16)
    normed[...] = half
    normed_t[...] = norm.T.astype(BF16)
    bricks, slots = send_rows.shape
    for brick in range(bricks):
        chosen = send_rows[brick : brick + 1, :]
        picks = (lax.broadcasted_iota(jnp.int32, (atoms, slots), 0) == chosen).astype(F32).astype(BF16)
        parcel[brick] = dot_tn(picks, half).astype(BF16)


def index_kernel(decay, neighbours, counts, distances, weight, absent, key_ref):
    slots, atoms = neighbours.shape
    heads, table_rows = weight.shape[:2]
    slot = lax.broadcasted_iota(jnp.int32, (slots, atoms), 0)
    valid = slot < counts[...]
    held = jnp.where(valid, neighbours[...], -1 - slot)
    rank = jnp.zeros((slots, atoms), jnp.int32)
    for j in range(slots):
        rank += ((held == held[j : j + 1, :]) & (slot > j)).astype(jnp.int32)
    key_ref[...] = jnp.where(valid, held + table_rows * rank, -1)
    weight[...] = jnp.zeros_like(weight)
    absent[...] = jnp.full_like(absent, -FAR)

    def layer(level, carry):
        for start in range(0, table_rows, CHUNK):
            at = pl.ds(start, CHUNK)
            row = lax.broadcasted_iota(jnp.int32, (CHUNK, atoms), 0) + (start + level * table_rows)
            distance = jnp.full((CHUNK, atoms), FAR, F32)
            for j in range(slots):
                distance = jnp.where(row == key_ref[j : j + 1, :], distances[j : j + 1, :], distance)
            absent[at, :] = jnp.where(distance < FAR, 0.0, absent[at, :])
            for h in range(heads):
                weight[h, at, :] += jnp.exp(-decay[h] * distance)
        return carry

    lax.fori_loop(0, jnp.max(rank) + 1, layer, 0)


def sweep_kernel(
    weights,
    normed,
    normed_t,
    ghosts,
    embedded,
    weight,
    absent,
    readout,
    targets,
    energies,
    grads,
    score_ref,
    att_ref,
    att_half,
    grad_score,
):
    atoms, width = normed.shape
    heads = weight.shape[0]
    head_size = width // heads
    scale = 1.0 / math.sqrt(head_size)
    head_of = lax.broadcasted_iota(jnp.int32, (atoms, width), 1) // head_size

    def stacked(array):
        zero = jnp.zeros_like(array)
        return jnp.concatenate([jnp.where(head_of == h, array, zero) for h in range(heads)], axis=0)

    def stacked_t(array):
        columns = []
        for h in range(heads):
            pieces = [array[h * head_size : (h + 1) * head_size]]
            if h > 0:
                pieces.insert(0, jnp.zeros((h * head_size, atoms), array.dtype))
            if h + 1 < heads:
                pieces.append(jnp.zeros((width - (h + 1) * head_size, atoms), array.dtype))
            columns.append(jnp.concatenate(pieces, axis=0))
        return jnp.concatenate(columns, axis=1)

    def own_channels(wide):
        return jnp.concatenate(
            [wide[h * head_size : (h + 1) * head_size, h * atoms : (h + 1) * atoms] for h in range(heads)], axis=0
        )

    norm = normed[...]
    table = jnp.concatenate([norm, ghosts[...]], axis=0)
    query = dot(norm, weights[0])
    keys = dot(table, weights[1]).astype(BF16)
    values = dot(table, weights[2]).astype(BF16)
    score_ref[...] = dot(keys, stacked_t(query.T.astype(BF16)))
    gone = absent[...]
    for h in range(heads):
        at = pl.ds(h * atoms, atoms)
        score = score_ref[:, at] * scale + gone
        terms = jnp.exp(score - jnp.max(score, axis=0, keepdims=True)) * weight[h]
        attention = terms * (1.0 / jnp.sum(terms, axis=0, keepdims=True))
        att_ref[:, at] = attention
        att_half[:, at] = attention.astype(BF16)
    attended_t = own_channels(dot_tn(values, att_half[...]))
    attended = attended_t.T.astype(BF16)

    out_proj = weights[3]
    updated = embedded[...] + dot(attended, out_proj)
    sigmoid = 1.0 / (1.0 + jnp.exp(-updated))
    energy = jnp.sum(readout[...] * (updated * sigmoid), axis=1, keepdims=True)
    energies[...] = to_row(energy)
    grad_energy = loss_weight * (energy - to_column(targets[...]))
    slope = sigmoid * (1.0 + updated * (1.0 - sigmoid))
    grad_updated = (grad_energy * readout[...] * slope).astype(BF16)
    grads[3] = dot(attended_t.astype(BF16), grad_updated)
    grad_attended = dot_nt(grad_updated, out_proj)

    score_ref[...] = dot(values, stacked_t(grad_attended.T.astype(BF16)))
    value_grads = dot(att_half[...], stacked(grad_attended.astype(BF16)))
    grads[2] = dot_tn(table, value_grads.astype(BF16))
    for h in range(heads):
        at = pl.ds(h * atoms, atoms)
        attention = att_ref[:, at]
        grad_weights = score_ref[:, at]
        mean = jnp.sum(attention * grad_weights, axis=0, keepdims=True)
        grad_score[:, at] = (attention * (grad_weights - mean)).astype(BF16)
    grad_query_t = own_channels(dot_tn(keys, grad_score[...])) * scale
    grads[0] = dot_nt(normed_t[...], grad_query_t.astype(BF16))
    key_grads = dot(grad_score[...], stacked(query.astype(BF16))) * scale
    grads[1] = dot_tn(table, key_grads.astype(BF16))


def vmem(count):
    return [pl.BlockSpec(memory_space=pltpu.VMEM)] * count


SMEM = pl.BlockSpec(memory_space=pltpu.SMEM)


def struct(shape, dtype):
    return jax.ShapeDtypeStruct(shape, dtype)


def flips(size, offset):
    return [(i, i ^ offset) for i in range(size)]


def halvings(size):
    offsets = []
    offset = size // 2
    while offset:
        offsets.append(offset)
        offset //= 2
    return offsets


def gather_cells(shard, cells):
    place = lax.axis_index("cell")
    offsets = halvings(cells)
    held = shard[None]
    for offset in offsets:
        other = lax.ppermute(held, "cell", flips(cells, offset))
        first = (place // offset) % 2 == 0
        held = jnp.where(first, jnp.concatenate([held, other]), jnp.concatenate([other, held]))
    bits = len(offsets)
    matrices, rows, width = shard.shape
    held = held.reshape((2,) * bits + shard.shape)
    held = held.transpose((bits,) + tuple(reversed(range(bits))) + (bits + 1, bits + 2))
    return held.reshape(matrices, cells * rows, width)


def reduce_cells(parts, cells):
    place = lax.axis_index("cell")
    tail = parts.shape[1:]
    for offset in reversed(halvings(cells)):
        bit = (place // offset) % 2
        pairs = parts.reshape((-1, 2) + tail)
        keep = lax.dynamic_index_in_dim(pairs, bit, 1, False)
        send = lax.dynamic_index_in_dim(pairs, 1 - bit, 1, False)
        parts = keep + lax.ppermute(send.astype(BF16), "cell", flips(cells, offset)).astype(F32)
    return parts[0]


def reduce_bricks(total, bricks):
    for offset in halvings(bricks):
        mine = total.astype(BF16)
        total = mine.astype(F32) + lax.ppermute(mine, "brick", flips(bricks, offset)).astype(F32)
    return total


def body(
    cells,
    bricks,
    features,
    species,
    species_table,
    neighbours,
    counts,
    send_lists,
    distances,
    head_decay,
    norm_gain,
    readout,
    targets,
    master,
    moment,
    second,
):
    atoms, width = features.shape[2:]
    slots = neighbours.shape[2]
    ghost_slots = send_lists.shape[3]
    heads = head_decay.shape[0]
    table_rows = atoms + bricks * ghost_slots

    weights = gather_cells(master.astype(BF16), cells)

    embedded, normed, normed_t, parcel = pl.pallas_call(
        embed_kernel,
        out_shape=(
            struct((atoms, width), F32),
            struct((atoms, width), BF16),
            struct((width, atoms), BF16),
            struct((bricks, ghost_slots, width), BF16),
        ),
        in_specs=vmem(5),
        out_specs=tuple(vmem(4)),
        name="embed",
    )(features[0, 0], species[0], species_table, norm_gain[None], send_lists[0, 0])

    brick = lax.axis_index("brick")
    ghosts = parcel
    for offset in range(1, bricks):
        peer = brick ^ offset
        sent = lax.dynamic_index_in_dim(parcel, peer, 0, True)
        arrived = lax.ppermute(sent, "brick", flips(bricks, offset))
        ghosts = lax.dynamic_update_slice_in_dim(ghosts, arrived, peer, 0)
    ghosts = ghosts.reshape(bricks * ghost_slots, width)

    weight, absent = pl.pallas_call(
        index_kernel,
        out_shape=(struct((heads, table_rows, atoms), F32), struct((table_rows, atoms), F32)),
        in_specs=[SMEM] + vmem(3),
        out_specs=tuple(vmem(2)),
        scratch_shapes=[pltpu.VMEM((slots, atoms), jnp.int32)],
        name="index",
    )(head_decay, neighbours[0, 0], counts[0], distances[0, 0])

    columns = heads * atoms
    energies, grads = pl.pallas_call(
        sweep_kernel,
        out_shape=(struct((1, atoms), F32), struct((4, width, width), F32)),
        in_specs=vmem(9),
        out_specs=tuple(vmem(2)),
        scratch_shapes=[
            pltpu.VMEM((table_rows, columns), F32),
            pltpu.VMEM((table_rows, columns), F32),
            pltpu.VMEM((table_rows, columns), BF16),
            pltpu.VMEM((table_rows, columns), BF16),
        ],
        compiler_params=pltpu.CompilerParams(vmem_limit_bytes=32 * 1024 * 1024),
        name="sweep",
    )(weights, normed, normed_t, ghosts, embedded, weight, absent, readout[None], targets[0])

    parts = grads.reshape(4, cells, width // cells, width).transpose(1, 0, 2, 3)
    owned = reduce_bricks(reduce_cells(parts, cells), bricks)
    moment_new = 0.9 * moment + 0.1 * owned
    second_new = 0.999 * second + 0.001 * owned * owned
    adam_step = moment_new / (jnp.sqrt(second_new) + 1e-08)
    return (energies[None], moment_new, second_new, adam_step)


def solution(mesh):
    return jax.shard_map(
        functools.partial(body, mesh.shape["cell"], mesh.shape["brick"]),
        mesh=mesh,
        in_specs=(
            P("cell", "brick", None, None),
            P("cell", "brick", None),
            P(),
            P("cell", "brick", None, None),
            P("cell", "brick", None),
            P("cell", "brick", None, None),
            P("cell", "brick", None, None),
            P(),
            P(),
            P(),
            P("cell", "brick", None),
            P(None, "cell", None),
            P(None, "cell", None),
            P(None, "cell", None),
        ),
        out_specs=(
            P("cell", "brick", None),
            P(None, "cell", None),
            P(None, "cell", None),
            P(None, "cell", None),
        ),
        check_vma=False,
    )
```

```python
import functools
import math

import jax
import jax.numpy as jnp
from jax import lax
from jax.experimental import pallas as pl
from jax.experimental.pallas import tpu as pltpu
from jax.sharding import PartitionSpec as P

CHUNK = 32
DEPTH = 5
FAR = 1e30

loss_weight = 0.0625
epsilon_norm = 1e-06

F32 = jnp.float32
BF16 = jnp.bfloat16
NT = (((1,), (1,)), ((), ()))
TN = (((0,), (0,)), ((), ()))


def dot(a, b):
    return jnp.dot(a, b, preferred_element_type=F32)


def dot_nt(a, b):
    return lax.dot_general(a, b, NT, preferred_element_type=F32)


def dot_tn(a, b):
    return lax.dot_general(a, b, TN, preferred_element_type=F32)


def to_column(row):
    n = row.shape[1]
    eye = lax.broadcasted_iota(jnp.int32, (n, n), 0) == lax.broadcasted_iota(jnp.int32, (n, n), 1)
    return jnp.sum(jnp.where(eye, row, jnp.zeros_like(row)), axis=1, keepdims=True)


def to_row(column):
    n = column.shape[0]
    eye = lax.broadcasted_iota(jnp.int32, (n, n), 0) == lax.broadcasted_iota(jnp.int32, (n, n), 1)
    return jnp.sum(jnp.where(eye, column, jnp.zeros_like(column)), axis=0, keepdims=True)


def embed_kernel(features, species, species_table, norm_gain, send_rows, embedded, normed, normed_t, parcel):
    atoms = features.shape[0]
    kinds = species_table.shape[0]
    column = to_column(species[...])
    total = features[...].astype(F32)
    picked = jnp.zeros_like(total)
    for kind in range(kinds):
        row = species_table[kind : kind + 1, :].astype(F32)
        picked = jnp.where(column == kind, row, picked)
    total = total + picked
    embedded[...] = total
    scale = lax.rsqrt(jnp.mean(total * total, axis=-1, keepdims=True) + epsilon_norm)
    norm = total * scale * norm_gain[...]
    half = norm.astype(BF16)
    normed[...] = half
    normed_t[...] = norm.T.astype(BF16)
    bricks, slots = send_rows.shape
    for brick in range(bricks):
        chosen = send_rows[brick : brick + 1, :]
        picks = (lax.broadcasted_iota(jnp.int32, (atoms, slots), 0) == chosen).astype(F32).astype(BF16)
        parcel[brick] = dot_tn(picks, half).astype(BF16)


def index_kernel(decay, neighbours, counts, distances, weight, absent, key_ref):
    slots, atoms = neighbours.shape
    heads, table_rows = weight.shape[:2]
    slot = lax.broadcasted_iota(jnp.int32, (slots, atoms), 0)
    valid = slot < counts[...]
    held = jnp.where(valid, neighbours[...], -1 - slot)
    key_ref[...] = held

    def chunk(step, nearest):
        start = pl.multiple_of(step * CHUNK, CHUNK)
        at = pl.ds(start, CHUNK)
        row = lax.broadcasted_iota(jnp.int32, (CHUNK, atoms), 0) + start
        layers = [jnp.full((CHUNK, atoms), FAR, F32) for _ in range(DEPTH)]
        for j in range(slots):
            hit = row == key_ref[j : j + 1, :]
            entering = distances[j : j + 1, :]
            for k in range(DEPTH):
                entering, layers[k] = layers[k], jnp.where(hit, entering, layers[k])
        absent[at, :] = jnp.where(layers[0] < FAR, 0.0, -FAR)
        for h in range(heads):
            weight[h, at, :] = sum(jnp.exp(-decay[h] * layer) for layer in layers)
        return jnp.minimum(nearest, jnp.min(layers[-1], axis=0, keepdims=True))

    nearest = lax.fori_loop(0, table_rows // CHUNK, chunk, jnp.full((1, atoms), FAR, F32))

    @pl.when(jnp.min(nearest) < FAR)
    def _():
        rank = jnp.zeros((slots, atoms), jnp.int32)
        for j in range(slots):
            rank += ((held == key_ref[j : j + 1, :]) & (slot < j)).astype(jnp.int32)
        key_ref[...] = jnp.where(valid, held + table_rows * rank, -1)

        def layer(level, carry):
            for start in range(0, table_rows, CHUNK):
                at = pl.ds(start, CHUNK)
                row = lax.broadcasted_iota(jnp.int32, (CHUNK, atoms), 0) + (start + level * table_rows)
                distance = jnp.full((CHUNK, atoms), FAR, F32)
                for j in range(slots):
                    distance = jnp.where(row == key_ref[j : j + 1, :], distances[j : j + 1, :], distance)
                for h in range(heads):
                    weight[h, at, :] += jnp.exp(-decay[h] * distance)
            return carry

        lax.fori_loop(DEPTH, jnp.max(rank) + 1, layer, 0)


def sweep_kernel(
    weights,
    normed,
    normed_t,
    ghosts,
    embedded,
    weight,
    absent,
    readout,
    targets,
    energies,
    grads,
    score_ref,
    att_ref,
    att_half,
    grad_score,
):
    atoms, width = normed.shape
    heads = weight.shape[0]
    head_size = width // heads
    scale = 1.0 / math.sqrt(head_size)
    head_of = lax.broadcasted_iota(jnp.int32, (atoms, width), 1) // head_size

    def stacked(array):
        zero = jnp.zeros_like(array)
        return jnp.concatenate([jnp.where(head_of == h, array, zero) for h in range(heads)], axis=0)

    def stacked_t(array):
        columns = []
        for h in range(heads):
            pieces = [array[h * head_size : (h + 1) * head_size]]
            if h > 0:
                pieces.insert(0, jnp.zeros((h * head_size, atoms), array.dtype))
            if h + 1 < heads:
                pieces.append(jnp.zeros((width - (h + 1) * head_size, atoms), array.dtype))
            columns.append(jnp.concatenate(pieces, axis=0))
        return jnp.concatenate(columns, axis=1)

    def own_channels(wide):
        return jnp.concatenate(
            [wide[h * head_size : (h + 1) * head_size, h * atoms : (h + 1) * atoms] for h in range(heads)], axis=0
        )

    norm = normed[...]
    table = jnp.concatenate([norm, ghosts[...]], axis=0)
    query = dot(norm, weights[0])
    keys = dot(table, weights[1]).astype(BF16)
    values = dot(table, weights[2]).astype(BF16)
    score_ref[...] = dot(keys, stacked_t(query.T.astype(BF16)))
    gone = absent[...]
    for h in range(heads):
        at = pl.ds(h * atoms, atoms)
        score = score_ref[:, at] * scale + gone
        terms = jnp.exp(score - jnp.max(score, axis=0, keepdims=True)) * weight[h]
        attention = terms * (1.0 / jnp.sum(terms, axis=0, keepdims=True))
        att_ref[:, at] = attention
        att_half[:, at] = attention.astype(BF16)
    attended_t = own_channels(dot_tn(values, att_half[...]))
    attended = attended_t.T.astype(BF16)

    out_proj = weights[3]
    updated = embedded[...] + dot(attended, out_proj)
    sigmoid = 1.0 / (1.0 + jnp.exp(-updated))
    energy = jnp.sum(readout[...] * (updated * sigmoid), axis=1, keepdims=True)
    energies[...] = to_row(energy)
    grad_energy = loss_weight * (energy - to_column(targets[...]))
    slope = sigmoid * (1.0 + updated * (1.0 - sigmoid))
    grad_updated = (grad_energy * readout[...] * slope).astype(BF16)
    grads[3] = dot(attended_t.astype(BF16), grad_updated)
    grad_attended = dot_nt(grad_updated, out_proj)

    score_ref[...] = dot(values, stacked_t(grad_attended.T.astype(BF16)))
    value_grads = dot(att_half[...], stacked(grad_attended.astype(BF16)))
    grads[2] = dot_tn(table, value_grads.astype(BF16))
    for h in range(heads):
        at = pl.ds(h * atoms, atoms)
        attention = att_ref[:, at]
        grad_weights = score_ref[:, at]
        mean = jnp.sum(attention * grad_weights, axis=0, keepdims=True)
        grad_score[:, at] = (attention * (grad_weights - mean)).astype(BF16)
    grad_query_t = own_channels(dot_tn(keys, grad_score[...])) * scale
    grads[0] = dot_nt(normed_t[...], grad_query_t.astype(BF16))
    key_grads = dot(grad_score[...], stacked(query.astype(BF16))) * scale
    grads[1] = dot_tn(table, key_grads.astype(BF16))


def vmem(count):
    return [pl.BlockSpec(memory_space=pltpu.VMEM)] * count


SMEM = pl.BlockSpec(memory_space=pltpu.SMEM)


def struct(shape, dtype):
    return jax.ShapeDtypeStruct(shape, dtype)


def pinned(shape, dtype):
    return pltpu.VMEM(shape, dtype)


def halvings(size):
    offsets = []
    offset = size // 2
    while offset:
        offsets.append(offset)
        offset //= 2
    return offsets


def crossing(offset, crossed):
    return offset | 1 if offset in crossed else offset


def own_core(cells, crossed):
    place = lax.axis_index("cell")
    blocks = 2 * jnp.arange(cells // 2)
    core = jnp.full((cells // 2,), place % 2)
    for offset in crossed:
        core = core ^ ((blocks // offset) % 2) ^ ((place // offset) % 2)
    return core


def swap(array, cells, vector_of):
    return lax.ppermute(array, "cell", [(i, i ^ vector_of(i)) for i in range(cells)])


def gather_cells(shard, cells, beside):
    place = lax.axis_index("cell")
    offsets = halvings(cells)[:-1]
    far, (a, b) = offsets[:-2], offsets[-2:]

    def late(i):
        return ((i // a) ^ (i // b) ^ i) % 2

    steps = [(offset, offset) for offset in far] + [(a, b), (b, a)]
    held = shard
    done = ()
    for early, other in steps:
        vectors = (crossing(early, offsets), crossing(other, offsets))
        arrived = swap(held, cells, lambda i, vectors=vectors: vectors[late(i)])
        if beside:
            done = beside.pop(0)(*done)
            arrived, done = lax.optimization_barrier((arrived, done))
        bit = jnp.where(late(place) == 0, place // early, place // other) % 2
        held = jnp.where(bit == 0, jnp.stack([held, arrived]), jnp.stack([arrived, held]))
    held = jnp.where(late(place) == 0, held, jnp.swapaxes(held, 0, 1))
    arrived = swap(held, cells, lambda i: 1)
    count = len(offsets)
    order = tuple(reversed(range(count))) + tuple(range(count, held.ndim))
    held, arrived = held.transpose(order), arrived.transpose(order)
    core = own_core(cells, offsets).reshape((2,) * count + (1,) * shard.ndim)
    pair = [jnp.where(core == 0, held, arrived), jnp.where(core == 0, arrived, held)]
    blocks = jnp.stack(pair, axis=count).reshape((cells,) + shard.shape)
    return blocks.transpose(1, 0, 2, 3).reshape(shard.shape[0], -1, shard.shape[2]), done


def reduce_all(parts, cells, bricks):
    place = lax.axis_index("cell")
    tail = parts.shape[1:]
    left = halvings(cells)[:-1]
    near, middle, farthest = left[-2:], left[1:-2], left[0]
    crossed = [near[0], *middle, farthest]
    parts = parts.reshape((cells // 2, 2) + tail)
    core = own_core(cells, crossed).reshape((cells // 2,) + (1,) * len(tail))
    keep = jnp.where(core == 0, parts[:, 0], parts[:, 1])
    send = jnp.where(core == 0, parts[:, 1], parts[:, 0])
    total = keep + swap(send.astype(BF16), cells, lambda i: 1).astype(F32)
    total = total.reshape((2,) * len(left) + tail)

    def portion(array, flipped):
        for offset, flip in reversed(flipped):
            bit = (place // offset) % 2
            array = lax.dynamic_index_in_dim(array, 1 - bit if flip else bit, left.index(offset), False)
        return array

    def exchange(group):
        nonlocal total, left
        mine = portion(total, [(offset, 0) for offset in group])
        for step in range(1, 1 << len(group)):
            flipped = [(offset, step >> k & 1) for k, offset in enumerate(group)]
            vector = 0
            for offset, flip in flipped:
                vector ^= crossing(offset, crossed) * flip
            sent = portion(total, flipped).astype(BF16)
            mine = mine + swap(sent, cells, lambda i, vector=vector: vector).astype(F32)
        total = mine
        left = [offset for offset in left if offset not in group]

    exchange(near)
    for offset in reversed(middle):
        exchange([offset])

    def meet(array, vector, step):
        pairs = [
            (cell * bricks + brick, (cell ^ vector) * bricks + (brick ^ step))
            for cell in range(cells)
            for brick in range(bricks)
        ]
        return lax.ppermute(array, ("cell", "brick"), pairs).astype(F32)

    vector = crossing(farthest, crossed)
    keep = portion(total, [(farthest, 0)]).astype(BF16)
    send = portion(total, [(farthest, 1)]).astype(BF16)
    total = keep.astype(F32) + meet(send, vector, 0)
    if bricks > 1:
        total = total + (meet(keep, 0, 1) + meet(send, vector, 1))
    for step in list(reversed(halvings(bricks)))[1:]:
        keep = total.astype(BF16)
        total = keep.astype(F32) + meet(keep, 0, step)
    return total


def body(
    cells,
    bricks,
    features,
    species,
    species_table,
    neighbours,
    counts,
    send_lists,
    distances,
    head_decay,
    norm_gain,
    readout,
    targets,
    master,
    moment,
    second,
):
    atoms, width = features.shape[2:]
    slots = neighbours.shape[2]
    ghost_slots = send_lists.shape[3]
    heads = head_decay.shape[0]
    table_rows = atoms + bricks * ghost_slots

    def embed():
        return pl.pallas_call(
            embed_kernel,
            out_shape=(
                pinned((atoms, width), F32),
                pinned((atoms, width), BF16),
                pinned((width, atoms), BF16),
                pinned((bricks, ghost_slots, width), BF16),
            ),
            in_specs=vmem(5),
            out_specs=tuple(vmem(4)),
            name="embed",
        )(features[0, 0], species[0], species_table, norm_gain[None], send_lists[0, 0])

    def exchange(embedded, normed, normed_t, parcel):
        brick = lax.axis_index("brick")
        ghosts = parcel
        for offset in range(1, bricks):
            peer = brick ^ offset
            sent = lax.dynamic_index_in_dim(parcel, peer, 0, True)
            arrived = lax.ppermute(sent, "brick", [(i, i ^ offset) for i in range(bricks)])
            ghosts = lax.dynamic_update_slice_in_dim(ghosts, arrived, peer, 0)
        return embedded, normed, normed_t, ghosts.reshape(bricks * ghost_slots, width)

    def index(*done):
        where = lax.optimization_barrier((done, neighbours))[1]
        return done + pl.pallas_call(
            index_kernel,
            out_shape=(pinned((heads, table_rows, atoms), F32), pinned((table_rows, atoms), F32)),
            in_specs=[SMEM] + vmem(3),
            out_specs=tuple(vmem(2)),
            scratch_shapes=[pltpu.VMEM((slots, atoms), jnp.int32)],
            name="index",
        )(head_decay, where[0, 0], counts[0], distances[0, 0])

    weights, done = gather_cells(master.astype(BF16), cells, [embed, exchange, index])
    embedded, normed, normed_t, ghosts, weight, absent = done

    columns = heads * atoms
    energies, grads = pl.pallas_call(
        sweep_kernel,
        out_shape=(struct((1, atoms), F32), struct((4, width, width), F32)),
        in_specs=vmem(9),
        out_specs=tuple(vmem(2)),
        scratch_shapes=[
            pltpu.VMEM((table_rows, columns), F32),
            pltpu.VMEM((table_rows, columns), F32),
            pltpu.VMEM((table_rows, columns), BF16),
            pltpu.VMEM((table_rows, columns), BF16),
        ],
        compiler_params=pltpu.CompilerParams(vmem_limit_bytes=32 * 1024 * 1024),
        name="sweep",
    )(weights, normed, normed_t, ghosts, embedded, weight, absent, readout[None], targets[0])

    parts = grads.reshape(4, cells, width // cells, width).transpose(1, 0, 2, 3)
    owned = reduce_all(parts, cells, bricks)
    moment_new = 0.9 * moment + 0.1 * owned
    second_new = 0.999 * second + 0.001 * owned * owned
    adam_step = moment_new / (jnp.sqrt(second_new) + 1e-08)
    return (energies[None], moment_new, second_new, adam_step)


def solution(mesh):
    return jax.shard_map(
        functools.partial(body, mesh.shape["cell"], mesh.shape["brick"]),
        mesh=mesh,
        in_specs=(
            P("cell", "brick", None, None),
            P("cell", "brick", None),
            P(),
            P("cell", "brick", None, None),
            P("cell", "brick", None),
            P("cell", "brick", None, None),
            P("cell", "brick", None, None),
            P(),
            P(),
            P(),
            P("cell", "brick", None),
            P(None, "cell", None),
            P(None, "cell", None),
            P(None, "cell", None),
        ),
        out_specs=(
            P("cell", "brick", None),
            P(None, "cell", None),
            P(None, "cell", None),
            P(None, "cell", None),
        ),
        check_vma=False,
    )
```

```python
import functools
import math

import jax
import jax.numpy as jnp
from jax import lax
from jax.experimental import pallas as pl
from jax.experimental.pallas import tpu as pltpu
from jax.sharding import PartitionSpec as P

CHUNK = 32
DEPTH = 5
FAR = 1e30
FAR_ROW = 1 << 20

loss_weight = 0.0625
epsilon_norm = 1e-06

F32 = jnp.float32
BF16 = jnp.bfloat16
NT = (((1,), (1,)), ((), ()))
TN = (((0,), (0,)), ((), ()))


def dot(a, b):
    return jnp.dot(a, b, preferred_element_type=F32)


def dot_nt(a, b):
    return lax.dot_general(a, b, NT, preferred_element_type=F32)


def dot_tn(a, b):
    return lax.dot_general(a, b, TN, preferred_element_type=F32)


def to_column(row):
    n = row.shape[1]
    eye = lax.broadcasted_iota(jnp.int32, (n, n), 0) == lax.broadcasted_iota(jnp.int32, (n, n), 1)
    return jnp.sum(jnp.where(eye, row, jnp.zeros_like(row)), axis=1, keepdims=True)


def to_row(column):
    n = column.shape[0]
    eye = lax.broadcasted_iota(jnp.int32, (n, n), 0) == lax.broadcasted_iota(jnp.int32, (n, n), 1)
    return jnp.sum(jnp.where(eye, column, jnp.zeros_like(column)), axis=0, keepdims=True)


def embed_kernel(features, species, species_table, norm_gain, send_rows, *refs):
    count = (len(refs) - 4) // 2
    embedded, normed, normed_t, parcel = refs[count : count + 4]
    for source, target in zip(refs[:count], refs[count + 4 :]):
        target[...] = source[...]
    atoms = features.shape[0]
    kinds = species_table.shape[0]
    column = to_column(species[...])
    total = features[...].astype(F32)
    picked = jnp.zeros_like(total)
    for kind in range(kinds):
        row = species_table[kind : kind + 1, :].astype(F32)
        picked = jnp.where(column == kind, row, picked)
    total = total + picked
    embedded[...] = total
    scale = lax.rsqrt(jnp.mean(total * total, axis=-1, keepdims=True) + epsilon_norm)
    norm = total * scale * norm_gain[...]
    half = norm.astype(BF16)
    normed[...] = half
    normed_t[...] = norm.T.astype(BF16)
    bricks, slots = send_rows.shape
    for brick in range(bricks):
        chosen = send_rows[brick : brick + 1, :]
        picks = (lax.broadcasted_iota(jnp.int32, (atoms, slots), 0) == chosen).astype(F32).astype(BF16)
        parcel[brick] = dot_tn(picks, half).astype(BF16)


def index_kernel(first, neighbours, counts, distances, decay, weight, absent, key_ref):
    slots, atoms = neighbours.shape
    heads, table_rows = weight.shape[:2]
    slot = lax.broadcasted_iota(jnp.int32, (slots, atoms), 0)
    valid = slot < counts[...]
    held = jnp.where(valid, neighbours[...] - first, -FAR_ROW - slot)
    key_ref[...] = held
    slope = [-decay[:, h : h + 1] for h in range(heads)]

    def chunk(step, nearest):
        start = pl.multiple_of(step * CHUNK, CHUNK)
        at = pl.ds(start, CHUNK)
        row = lax.broadcasted_iota(jnp.int32, (CHUNK, atoms), 0) + start
        layers = [jnp.full((CHUNK, atoms), FAR, F32) for _ in range(DEPTH)]
        for j in range(slots):
            hit = row == key_ref[j : j + 1, :]
            entering = distances[j : j + 1, :]
            for k in range(DEPTH):
                entering, layers[k] = layers[k], jnp.where(hit, entering, layers[k])
        absent[at, :] = jnp.where(layers[0] < FAR, 0.0, -FAR)
        for h in range(heads):
            weight[h, at, :] = sum(jnp.exp(slope[h] * layer) for layer in layers)
        return jnp.minimum(nearest, jnp.min(layers[-1], axis=0, keepdims=True))

    nearest = lax.fori_loop(0, table_rows // CHUNK, chunk, jnp.full((1, atoms), FAR, F32))

    @pl.when(jnp.min(nearest) < FAR)
    def _():
        rank = jnp.zeros((slots, atoms), jnp.int32)
        for j in range(slots):
            rank += ((held == key_ref[j : j + 1, :]) & (slot < j)).astype(jnp.int32)
        inside = valid & (held >= 0) & (held < table_rows)
        key_ref[...] = jnp.where(inside, held + table_rows * rank, -1)

        def layer(level, carry):
            for start in range(0, table_rows, CHUNK):
                at = pl.ds(start, CHUNK)
                row = lax.broadcasted_iota(jnp.int32, (CHUNK, atoms), 0) + (start + level * table_rows)
                distance = jnp.full((CHUNK, atoms), FAR, F32)
                for j in range(slots):
                    distance = jnp.where(row == key_ref[j : j + 1, :], distances[j : j + 1, :], distance)
                for h in range(heads):
                    weight[h, at, :] += jnp.exp(slope[h] * distance)
            return carry

        lax.fori_loop(DEPTH, jnp.max(rank) + 1, layer, 0)


def sweep_kernel(
    weights,
    normed,
    normed_t,
    ghosts,
    embedded,
    weight,
    absent,
    weight_rest,
    absent_rest,
    readout,
    targets,
    energies,
    grads,
    score_ref,
    att_ref,
    att_half,
    grad_score,
):
    atoms, width = normed.shape
    heads = weight.shape[0]
    head_size = width // heads
    scale = 1.0 / math.sqrt(head_size)
    head_of = lax.broadcasted_iota(jnp.int32, (atoms, width), 1) // head_size

    def stacked(array):
        zero = jnp.zeros_like(array)
        return jnp.concatenate([jnp.where(head_of == h, array, zero) for h in range(heads)], axis=0)

    def stacked_t(array):
        columns = []
        for h in range(heads):
            pieces = [array[h * head_size : (h + 1) * head_size]]
            if h > 0:
                pieces.insert(0, jnp.zeros((h * head_size, atoms), array.dtype))
            if h + 1 < heads:
                pieces.append(jnp.zeros((width - (h + 1) * head_size, atoms), array.dtype))
            columns.append(jnp.concatenate(pieces, axis=0))
        return jnp.concatenate(columns, axis=1)

    def own_channels(wide):
        return jnp.concatenate(
            [wide[h * head_size : (h + 1) * head_size, h * atoms : (h + 1) * atoms] for h in range(heads)], axis=0
        )

    norm = normed[...]
    table = jnp.concatenate([norm, ghosts[...]], axis=0)
    query = dot(norm, weights[0])
    keys = dot(table, weights[1]).astype(BF16)
    values = dot(table, weights[2]).astype(BF16)
    score_ref[...] = dot(keys, stacked_t(query.T.astype(BF16)))
    gone = jnp.concatenate([absent[...], absent_rest[...]], axis=0)
    for h in range(heads):
        at = pl.ds(h * atoms, atoms)
        score = score_ref[:, at] * scale + gone
        weights_h = jnp.concatenate([weight[h], weight_rest[h]], axis=0)
        terms = jnp.exp(score - jnp.max(score, axis=0, keepdims=True)) * weights_h
        attention = terms * (1.0 / jnp.sum(terms, axis=0, keepdims=True))
        att_ref[:, at] = attention
        att_half[:, at] = attention.astype(BF16)
    attended_t = own_channels(dot_tn(values, att_half[...]))
    attended = attended_t.T.astype(BF16)

    out_proj = weights[3]
    updated = embedded[...] + dot(attended, out_proj)
    sigmoid = 1.0 / (1.0 + jnp.exp(-updated))
    energy = jnp.sum(readout[...] * (updated * sigmoid), axis=1, keepdims=True)
    energies[...] = to_row(energy)
    grad_energy = loss_weight * (energy - to_column(targets[...]))
    slope = sigmoid * (1.0 + updated * (1.0 - sigmoid))
    grad_updated = (grad_energy * readout[...] * slope).astype(BF16)
    grads[3] = dot(attended_t.astype(BF16), grad_updated)
    grad_attended = dot_nt(grad_updated, out_proj)

    score_ref[...] = dot(values, stacked_t(grad_attended.T.astype(BF16)))
    value_grads = dot(att_half[...], stacked(grad_attended.astype(BF16)))
    grads[2] = dot_tn(table, value_grads.astype(BF16))
    for h in range(heads):
        at = pl.ds(h * atoms, atoms)
        attention = att_ref[:, at]
        grad_weights = score_ref[:, at]
        mean = jnp.sum(attention * grad_weights, axis=0, keepdims=True)
        grad_score[:, at] = (attention * (grad_weights - mean)).astype(BF16)
    grad_query_t = own_channels(dot_tn(keys, grad_score[...])) * scale
    grads[0] = dot_nt(normed_t[...], grad_query_t.astype(BF16))
    key_grads = dot(grad_score[...], stacked(query.astype(BF16))) * scale
    grads[1] = dot_tn(table, key_grads.astype(BF16))


def vmem(count):
    return [pl.BlockSpec(memory_space=pltpu.VMEM)] * count


SMEM = pl.BlockSpec(memory_space=pltpu.SMEM)


def struct(shape, dtype):
    return jax.ShapeDtypeStruct(shape, dtype)


def pinned(shape, dtype):
    return pltpu.VMEM(shape, dtype)


def halvings(size):
    offsets = []
    offset = size // 2
    while offset:
        offsets.append(offset)
        offset //= 2
    return offsets


def crossing(offset, crossed):
    return offset | 1 if offset in crossed else offset


def own_core(cells, crossed):
    place = lax.axis_index("cell")
    blocks = 2 * jnp.arange(cells // 2)
    core = jnp.full((cells // 2,), place % 2)
    for offset in crossed:
        core = core ^ ((blocks // offset) % 2) ^ ((place // offset) % 2)
    return core


def swap(array, cells, vector_of):
    return lax.ppermute(array, "cell", [(i, i ^ vector_of(i)) for i in range(cells)])


def gather_cells(shard, cells, beside):
    place = lax.axis_index("cell")
    offsets = halvings(cells)[:-1]
    far, (a, b) = offsets[:-2], offsets[-2:]

    def late(i):
        return ((i // a) ^ (i // b) ^ i) % 2

    steps = [(offset, offset) for offset in far] + [(a, b), (b, a)]
    held = shard
    done = ()
    for early, other in steps:
        vectors = (crossing(early, offsets), crossing(other, offsets))
        work = beside.pop(0)(*done) if beside else done
        arrived = swap(held, cells, lambda i, vectors=vectors: vectors[late(i)])
        done, arrived = lax.optimization_barrier((work, arrived))
        bit = jnp.where(late(place) == 0, place // early, place // other) % 2
        held = jnp.where(bit == 0, jnp.stack([held, arrived]), jnp.stack([arrived, held]))
    held = jnp.where(late(place) == 0, held, jnp.swapaxes(held, 0, 1))
    arrived = swap(held, cells, lambda i: 1)
    count = len(offsets)
    order = tuple(reversed(range(count))) + tuple(range(count, held.ndim))
    held, arrived = held.transpose(order), arrived.transpose(order)
    core = own_core(cells, offsets).reshape((2,) * count + (1,) * shard.ndim)
    pair = [jnp.where(core == 0, held, arrived), jnp.where(core == 0, arrived, held)]
    blocks = jnp.stack(pair, axis=count).reshape((cells,) + shard.shape)
    return blocks.transpose(1, 0, 2, 3).reshape(shard.shape[0], -1, shard.shape[2]), done


def reduce_all(parts, cells, bricks):
    place = lax.axis_index("cell")
    tail = parts.shape[1:]
    left = halvings(cells)[:-1]
    near, middle, farthest = left[-2:], left[1:-2], left[0]
    crossed = [near[0], *middle, farthest]
    parts = parts.reshape((cells // 2, 2) + tail)
    core = own_core(cells, crossed).reshape((cells // 2,) + (1,) * len(tail))
    keep = jnp.where(core == 0, parts[:, 0], parts[:, 1])
    send = jnp.where(core == 0, parts[:, 1], parts[:, 0])
    total = keep + swap(send.astype(BF16), cells, lambda i: 1).astype(F32)
    total = total.reshape((2,) * len(left) + tail)

    def portion(array, flipped):
        for offset, flip in reversed(flipped):
            bit = (place // offset) % 2
            array = lax.dynamic_index_in_dim(array, 1 - bit if flip else bit, left.index(offset), False)
        return array

    def exchange(group):
        nonlocal total, left
        mine = portion(total, [(offset, 0) for offset in group])
        for step in range(1, 1 << len(group)):
            flipped = [(offset, step >> k & 1) for k, offset in enumerate(group)]
            vector = 0
            for offset, flip in flipped:
                vector ^= crossing(offset, crossed) * flip
            sent = portion(total, flipped).astype(BF16)
            mine = mine + swap(sent, cells, lambda i, vector=vector: vector).astype(F32)
        total = mine
        left = [offset for offset in left if offset not in group]

    exchange(near)
    for offset in reversed(middle):
        exchange([offset])

    def meet(array, vector, step):
        pairs = [
            (cell * bricks + brick, (cell ^ vector) * bricks + (brick ^ step))
            for cell in range(cells)
            for brick in range(bricks)
        ]
        return lax.ppermute(array, ("cell", "brick"), pairs).astype(F32)

    vector = crossing(farthest, crossed)
    keep = portion(total, [(farthest, 0)]).astype(BF16)
    send = portion(total, [(farthest, 1)]).astype(BF16)
    total = keep.astype(F32) + meet(send, vector, 0)
    if bricks > 1:
        far = meet(send, vector, 1)
        total = total + (far + meet(keep, 0, 1))
    for step in list(reversed(halvings(bricks)))[1:]:
        keep = total.astype(BF16)
        total = keep.astype(F32) + meet(keep, 0, step)
    return total


def body(
    cells,
    bricks,
    features,
    species,
    species_table,
    neighbours,
    counts,
    send_lists,
    distances,
    head_decay,
    norm_gain,
    readout,
    targets,
    master,
    moment,
    second,
):
    atoms, width = features.shape[2:]
    slots = neighbours.shape[2]
    ghost_slots = send_lists.shape[3]
    heads = head_decay.shape[0]
    table_rows = atoms + bricks * ghost_slots

    kept = (neighbours[0, 0], counts[0], distances[0, 0], head_decay[None], readout[None], targets[0])

    def embed():
        return pl.pallas_call(
            embed_kernel,
            out_shape=(
                pinned((atoms, width), F32),
                pinned((atoms, width), BF16),
                pinned((width, atoms), BF16),
                pinned((bricks, ghost_slots, width), BF16),
                *(pinned(array.shape, array.dtype) for array in kept),
            ),
            in_specs=vmem(5 + len(kept)),
            out_specs=tuple(vmem(4 + len(kept))),
            compiler_params=pltpu.CompilerParams(vmem_limit_bytes=4 * 1024 * 1024),
            name="embed",
        )(features[0, 0], species[0], species_table, norm_gain[None], send_lists[0, 0], *kept)

    def exchange(embedded, normed, normed_t, parcel):
        brick = lax.axis_index("brick")
        ghosts = parcel
        for offset in range(1, bricks):
            peer = brick ^ offset
            sent = lax.dynamic_index_in_dim(parcel, peer, 0, True)
            arrived = lax.ppermute(sent, "brick", [(i, i ^ offset) for i in range(bricks)])
            ghosts = lax.dynamic_update_slice_in_dim(ghosts, arrived, peer, 0)
        return embedded, normed, normed_t, ghosts.reshape(bricks * ghost_slots, width)

    part = table_rows // 2

    def index(first, rows, valid, away, decay):
        return pl.pallas_call(
            functools.partial(index_kernel, first),
            out_shape=(pinned((heads, part, atoms), F32), pinned((part, atoms), F32)),
            in_specs=vmem(4),
            out_specs=tuple(vmem(2)),
            scratch_shapes=[pltpu.VMEM((slots, atoms), jnp.int32)],
            compiler_params=pltpu.CompilerParams(vmem_limit_bytes=8 * 1024 * 1024),
            name="index",
        )(rows, valid, away, decay)

    def prepare():
        done = embed()
        return done[:4], done[4:8], done[8:], index(0, *done[4:8])

    ghosts = []

    def send(state, slot_arrays, held, half):
        ghosts.append(exchange(*state))
        return state, slot_arrays, held, half

    def finish(state, slot_arrays, held, half):
        return ghosts[0], held, half, index(part, *slot_arrays)

    weights, done = gather_cells(master.astype(BF16), cells, [prepare, send, finish])
    (embedded, normed, normed_t, ghosts), held, *halves = done

    columns = heads * atoms
    energies, grads = pl.pallas_call(
        sweep_kernel,
        out_shape=(struct((1, atoms), F32), struct((4, width, width), F32)),
        in_specs=vmem(11),
        out_specs=tuple(vmem(2)),
        scratch_shapes=[
            pltpu.VMEM((table_rows, columns), F32),
            pltpu.VMEM((table_rows, columns), F32),
            pltpu.VMEM((table_rows, columns), BF16),
            pltpu.VMEM((table_rows, columns), BF16),
        ],
        compiler_params=pltpu.CompilerParams(vmem_limit_bytes=32 * 1024 * 1024),
        name="sweep",
    )(weights, normed, normed_t, ghosts, embedded, *halves[0], *halves[1], *held)

    parts = grads.reshape(4, cells, width // cells, width).transpose(1, 0, 2, 3)
    owned = reduce_all(parts, cells, bricks)
    moment_new = 0.9 * moment + 0.1 * owned
    second_new = 0.999 * second + 0.001 * owned * owned
    adam_step = moment_new / (jnp.sqrt(second_new) + 1e-08)
    return (energies[None], moment_new, second_new, adam_step)


def solution(mesh):
    return jax.shard_map(
        functools.partial(body, mesh.shape["cell"], mesh.shape["brick"]),
        mesh=mesh,
        in_specs=(
            P("cell", "brick", None, None),
            P("cell", "brick", None),
            P(),
            P("cell", "brick", None, None),
            P("cell", "brick", None),
            P("cell", "brick", None, None),
            P("cell", "brick", None, None),
            P(),
            P(),
            P(),
            P("cell", "brick", None),
            P(None, "cell", None),
            P(None, "cell", None),
            P(None, "cell", None),
        ),
        out_specs=(
            P("cell", "brick", None),
            P(None, "cell", None),
            P(None, "cell", None),
            P(None, "cell", None),
        ),
        check_vma=False,
    )
```

```python
import functools
import math

import jax
import jax.numpy as jnp
from jax import lax
from jax.experimental import pallas as pl
from jax.experimental.pallas import tpu as pltpu
from jax.sharding import PartitionSpec as P

CHUNK = 32
DEPTH = 5
FAR = 1e30
FAR_ROW = 1 << 20

loss_weight = 0.0625
epsilon_norm = 1e-06

F32 = jnp.float32
BF16 = jnp.bfloat16
NT = (((1,), (1,)), ((), ()))
TN = (((0,), (0,)), ((), ()))


def dot(a, b):
    return jnp.dot(a, b, preferred_element_type=F32)


def dot_nt(a, b):
    return lax.dot_general(a, b, NT, preferred_element_type=F32)


def dot_tn(a, b):
    return lax.dot_general(a, b, TN, preferred_element_type=F32)


def to_column(row):
    n = row.shape[1]
    eye = lax.broadcasted_iota(jnp.int32, (n, n), 0) == lax.broadcasted_iota(jnp.int32, (n, n), 1)
    return jnp.sum(jnp.where(eye, row, jnp.zeros_like(row)), axis=1, keepdims=True)


def to_row(column):
    n = column.shape[0]
    eye = lax.broadcasted_iota(jnp.int32, (n, n), 0) == lax.broadcasted_iota(jnp.int32, (n, n), 1)
    return jnp.sum(jnp.where(eye, column, jnp.zeros_like(column)), axis=0, keepdims=True)


def embed_kernel(features, species, species_table, norm_gain, send_rows, *refs):
    count = (len(refs) - 4) // 2
    embedded, normed, normed_t, parcel = refs[count : count + 4]
    for source, target in zip(refs[:count], refs[count + 4 :]):
        target[...] = source[...]
    atoms = features.shape[0]
    kinds = species_table.shape[0]
    column = to_column(species[...])
    total = features[...].astype(F32)
    picked = jnp.zeros_like(total)
    for kind in range(kinds):
        row = species_table[kind : kind + 1, :].astype(F32)
        picked = jnp.where(column == kind, row, picked)
    total = total + picked
    embedded[...] = total
    scale = lax.rsqrt(jnp.mean(total * total, axis=-1, keepdims=True) + epsilon_norm)
    norm = total * scale * norm_gain[...]
    half = norm.astype(BF16)
    normed[...] = half
    normed_t[...] = norm.T.astype(BF16)
    bricks, slots = send_rows.shape
    for brick in range(bricks):
        chosen = send_rows[brick : brick + 1, :]
        picks = (lax.broadcasted_iota(jnp.int32, (atoms, slots), 0) == chosen).astype(F32).astype(BF16)
        parcel[brick] = dot_tn(picks, half).astype(BF16)


def index_kernel(first, neighbours, counts, distances, decay, weight, absent, key_ref):
    slots, atoms = neighbours.shape
    heads, table_rows = weight.shape[:2]
    slot = lax.broadcasted_iota(jnp.int32, (slots, atoms), 0)
    valid = slot < counts[...]
    held = jnp.where(valid, neighbours[...] - first, -FAR_ROW - slot)
    key_ref[...] = held
    slope = [-decay[:, h : h + 1] for h in range(heads)]

    def chunk(step, nearest):
        start = pl.multiple_of(step * CHUNK, CHUNK)
        at = pl.ds(start, CHUNK)
        row = lax.broadcasted_iota(jnp.int32, (CHUNK, atoms), 0) + start
        layers = [jnp.full((CHUNK, atoms), FAR, F32) for _ in range(DEPTH)]
        for j in range(slots):
            hit = row == key_ref[j : j + 1, :]
            entering = distances[j : j + 1, :]
            for k in range(DEPTH):
                entering, layers[k] = layers[k], jnp.where(hit, entering, layers[k])
        absent[at, :] = jnp.where(layers[0] < FAR, 0.0, -FAR)
        for h in range(heads):
            weight[h, at, :] = sum(jnp.exp(slope[h] * layer) for layer in layers)
        return jnp.minimum(nearest, jnp.min(layers[-1], axis=0, keepdims=True))

    nearest = lax.fori_loop(0, table_rows // CHUNK, chunk, jnp.full((1, atoms), FAR, F32))

    @pl.when(jnp.min(nearest) < FAR)
    def _():
        rank = jnp.zeros((slots, atoms), jnp.int32)
        for j in range(slots):
            rank += ((held == key_ref[j : j + 1, :]) & (slot < j)).astype(jnp.int32)
        inside = valid & (held >= 0) & (held < table_rows)
        key_ref[...] = jnp.where(inside, held + table_rows * rank, -1)

        def layer(level, carry):
            for start in range(0, table_rows, CHUNK):
                at = pl.ds(start, CHUNK)
                row = lax.broadcasted_iota(jnp.int32, (CHUNK, atoms), 0) + (start + level * table_rows)
                distance = jnp.full((CHUNK, atoms), FAR, F32)
                for j in range(slots):
                    distance = jnp.where(row == key_ref[j : j + 1, :], distances[j : j + 1, :], distance)
                for h in range(heads):
                    weight[h, at, :] += jnp.exp(slope[h] * distance)
            return carry

        lax.fori_loop(DEPTH, jnp.max(rank) + 1, layer, 0)


def sweep_kernel(
    weights,
    normed,
    normed_t,
    ghosts,
    embedded,
    weight,
    absent,
    weight_rest,
    absent_rest,
    readout,
    targets,
    energies,
    grads,
    score_ref,
    att_ref,
    att_half,
    grad_score,
):
    atoms, width = normed.shape
    heads = weight.shape[0]
    head_size = width // heads
    scale = 1.0 / math.sqrt(head_size)
    head_of = lax.broadcasted_iota(jnp.int32, (atoms, width), 1) // head_size

    def stacked(array):
        zero = jnp.zeros_like(array)
        return jnp.concatenate([jnp.where(head_of == h, array, zero) for h in range(heads)], axis=0)

    def stacked_t(array):
        columns = []
        for h in range(heads):
            pieces = [array[h * head_size : (h + 1) * head_size]]
            if h > 0:
                pieces.insert(0, jnp.zeros((h * head_size, atoms), array.dtype))
            if h + 1 < heads:
                pieces.append(jnp.zeros((width - (h + 1) * head_size, atoms), array.dtype))
            columns.append(jnp.concatenate(pieces, axis=0))
        return jnp.concatenate(columns, axis=1)

    def own_channels(wide):
        return jnp.concatenate(
            [wide[h * head_size : (h + 1) * head_size, h * atoms : (h + 1) * atoms] for h in range(heads)], axis=0
        )

    norm = normed[...]
    table = jnp.concatenate([norm, ghosts[...]], axis=0)
    query = dot(norm, weights[0])
    keys = dot(table, weights[1]).astype(BF16)
    values = dot(table, weights[2]).astype(BF16)
    score_ref[...] = dot(keys, stacked_t(query.T.astype(BF16)))
    gone = jnp.concatenate([absent[...], absent_rest[...]], axis=0)
    for h in range(heads):
        at = pl.ds(h * atoms, atoms)
        score = score_ref[:, at] * scale + gone
        weights_h = jnp.concatenate([weight[h], weight_rest[h]], axis=0)
        terms = jnp.exp(score - jnp.max(score, axis=0, keepdims=True)) * weights_h
        attention = terms * (1.0 / jnp.sum(terms, axis=0, keepdims=True))
        att_ref[:, at] = attention
        att_half[:, at] = attention.astype(BF16)
    attended_t = own_channels(dot_tn(values, att_half[...]))
    attended = attended_t.T.astype(BF16)

    out_proj = weights[3]
    updated = embedded[...] + dot(attended, out_proj)
    sigmoid = 1.0 / (1.0 + jnp.exp(-updated))
    energy = jnp.sum(readout[...] * (updated * sigmoid), axis=1, keepdims=True)
    energies[...] = to_row(energy)
    grad_energy = loss_weight * (energy - to_column(targets[...]))
    slope = sigmoid * (1.0 + updated * (1.0 - sigmoid))
    grad_updated = (grad_energy * readout[...] * slope).astype(BF16)
    grads[3] = dot(attended_t.astype(BF16), grad_updated)
    grad_attended = dot_nt(grad_updated, out_proj)

    score_ref[...] = dot(values, stacked_t(grad_attended.T.astype(BF16)))
    value_grads = dot(att_half[...], stacked(grad_attended.astype(BF16)))
    grads[2] = dot_tn(table, value_grads.astype(BF16))
    for h in range(heads):
        at = pl.ds(h * atoms, atoms)
        attention = att_ref[:, at]
        grad_weights = score_ref[:, at]
        mean = jnp.sum(attention * grad_weights, axis=0, keepdims=True)
        grad_score[:, at] = (attention * (grad_weights - mean)).astype(BF16)
    grad_query_t = own_channels(dot_tn(keys, grad_score[...])) * scale
    grads[0] = dot_nt(normed_t[...], grad_query_t.astype(BF16))
    key_grads = dot(grad_score[...], stacked(query.astype(BF16))) * scale
    grads[1] = dot_tn(table, key_grads.astype(BF16))


def vmem(count):
    return [pl.BlockSpec(memory_space=pltpu.VMEM)] * count


SMEM = pl.BlockSpec(memory_space=pltpu.SMEM)


def struct(shape, dtype):
    return jax.ShapeDtypeStruct(shape, dtype)


def pinned(shape, dtype):
    return pltpu.VMEM(shape, dtype)


def halvings(size):
    offsets = []
    offset = size // 2
    while offset:
        offsets.append(offset)
        offset //= 2
    return offsets


def crossing(offset, crossed):
    return offset | 1 if offset in crossed else offset


def own_core(cells, crossed):
    place = lax.axis_index("cell")
    blocks = 2 * jnp.arange(cells // 2)
    core = jnp.full((cells // 2,), place % 2)
    for offset in crossed:
        core = core ^ ((blocks // offset) % 2) ^ ((place // offset) % 2)
    return core


def swap(array, cells, vector_of):
    return lax.ppermute(array, "cell", [(i, i ^ vector_of(i)) for i in range(cells)])


def gather_cells(shard, cells, beside, first):
    place = lax.axis_index("cell")
    offsets = halvings(cells)[:-1]
    far, (a, b) = offsets[:-2], offsets[-2:]
    crossed = [*far, b]
    held = shard
    done = ()

    def step(vectors, after=None):
        nonlocal done
        work = beside.pop(0)(*done) if beside else done
        arrived = [swap(held, cells, lambda i, vector=vector: vector) for vector in vectors]
        if after is not None:
            arrived[0], early = after(arrived[0])
            work = (*work, early)
        done, arrived = lax.optimization_barrier((work, arrived))
        return arrived

    def placed(first, second, offset):
        own = (place // offset) % 2 == 0
        return jnp.where(own, jnp.stack([first, second]), jnp.stack([second, first]))

    for offset in far:
        held = placed(held, step([crossing(offset, crossed)])[0], offset)
    vectors = [crossing(offset, crossed) for offset in (a, b)]
    over_both, over_a, over_b = step([vectors[0] ^ vectors[1], *vectors], first)
    held = placed(placed(held, over_b, b), placed(over_a, over_both, b), a)
    (arrived,) = step([1])
    count = len(offsets)
    order = (*reversed(range(2, count)), 0, 1, *range(count, held.ndim))
    held, arrived = held.transpose(order), arrived.transpose(order)
    core = own_core(cells, crossed).reshape((2,) * count + (1,) * shard.ndim)
    pair = [jnp.where(core == 0, held, arrived), jnp.where(core == 0, arrived, held)]
    blocks = jnp.stack(pair, axis=count).reshape((cells,) + shard.shape)
    return blocks.transpose(1, 0, 2, 3).reshape(shard.shape[0], -1, shard.shape[2]), done


def reduce_all(parts, cells, bricks):
    place = lax.axis_index("cell")
    tail = parts.shape[1:]
    left = halvings(cells)[:-1]
    near, middle, farthest = left[-2:], left[1:-2], left[0]
    crossed = [near[0], *middle, farthest]
    parts = parts.reshape((cells // 2, 2) + tail)
    core = own_core(cells, crossed).reshape((cells // 2,) + (1,) * len(tail))
    keep = jnp.where(core == 0, parts[:, 0], parts[:, 1])
    send = jnp.where(core == 0, parts[:, 1], parts[:, 0])
    total = keep + swap(send.astype(BF16), cells, lambda i: 1).astype(F32)
    total = total.reshape((2,) * len(left) + tail)

    def portion(array, flipped):
        for offset, flip in reversed(flipped):
            bit = (place // offset) % 2
            array = lax.dynamic_index_in_dim(array, 1 - bit if flip else bit, left.index(offset), False)
        return array

    def exchange(group):
        nonlocal total, left
        mine = portion(total, [(offset, 0) for offset in group])
        for step in range(1, 1 << len(group)):
            flipped = [(offset, step >> k & 1) for k, offset in enumerate(group)]
            vector = 0
            for offset, flip in flipped:
                vector ^= crossing(offset, crossed) * flip
            sent = portion(total, flipped).astype(BF16)
            mine = mine + swap(sent, cells, lambda i, vector=vector: vector).astype(F32)
        total = mine
        left = [offset for offset in left if offset not in group]

    exchange(near)
    for offset in reversed(middle):
        exchange([offset])

    def meet(array, vector, step):
        pairs = [
            (cell * bricks + brick, (cell ^ vector) * bricks + (brick ^ step))
            for cell in range(cells)
            for brick in range(bricks)
        ]
        return lax.ppermute(array, ("cell", "brick"), pairs).astype(F32)

    vector = crossing(farthest, crossed)
    keep = portion(total, [(farthest, 0)]).astype(BF16)
    send = portion(total, [(farthest, 1)]).astype(BF16)
    total = keep.astype(F32) + meet(send, vector, 0)
    if bricks > 1:
        far = meet(send, vector, 1)
        total = total + (far + meet(keep, 0, 1))
    for step in list(reversed(halvings(bricks)))[1:]:
        keep = total.astype(BF16)
        total = keep.astype(F32) + meet(keep, 0, step)
    return total


def body(
    cells,
    bricks,
    features,
    species,
    species_table,
    neighbours,
    counts,
    send_lists,
    distances,
    head_decay,
    norm_gain,
    readout,
    targets,
    master,
    moment,
    second,
):
    atoms, width = features.shape[2:]
    slots = neighbours.shape[2]
    ghost_slots = send_lists.shape[3]
    heads = head_decay.shape[0]
    table_rows = atoms + bricks * ghost_slots

    kept = (neighbours[0, 0], counts[0], distances[0, 0], head_decay[None], readout[None], targets[0])

    def embed():
        return pl.pallas_call(
            embed_kernel,
            out_shape=(
                pinned((atoms, width), F32),
                pinned((atoms, width), BF16),
                pinned((width, atoms), BF16),
                pinned((bricks, ghost_slots, width), BF16),
                *(pinned(array.shape, array.dtype) for array in kept),
            ),
            in_specs=vmem(5 + len(kept)),
            out_specs=tuple(vmem(4 + len(kept))),
            compiler_params=pltpu.CompilerParams(vmem_limit_bytes=4 * 1024 * 1024),
            name="embed",
        )(features[0, 0], species[0], species_table, norm_gain[None], send_lists[0, 0], *kept)

    def exchange(embedded, normed, normed_t, parcel):
        brick = lax.axis_index("brick")
        ghosts = parcel
        for offset in range(1, bricks):
            peer = brick ^ offset
            sent = lax.dynamic_index_in_dim(parcel, peer, 0, True)
            arrived = lax.ppermute(sent, "brick", [(i, i ^ offset) for i in range(bricks)])
            ghosts = lax.dynamic_update_slice_in_dim(ghosts, arrived, peer, 0)
        return embedded, normed, normed_t, ghosts.reshape(bricks * ghost_slots, width)

    part = table_rows // 2

    def index(first, rows, valid, away, decay):
        return pl.pallas_call(
            functools.partial(index_kernel, first),
            out_shape=(pinned((heads, part, atoms), F32), pinned((part, atoms), F32)),
            in_specs=vmem(4),
            out_specs=tuple(vmem(2)),
            scratch_shapes=[pltpu.VMEM((slots, atoms), jnp.int32)],
            compiler_params=pltpu.CompilerParams(vmem_limit_bytes=8 * 1024 * 1024),
            name="index",
        )(rows, valid, away, decay)

    def prepare():
        done = embed()
        return done[:4], done[4:8], done[8:], index(0, *done[4:8])

    ghosts = []

    def send(state, slot_arrays, held, half):
        ghosts.append(state)
        return held, half, index(part, *slot_arrays)

    def start(arrived):
        return arrived, exchange(*ghosts.pop())

    def receive(held, half, rest, state):
        return state, held, half, rest

    steps = [prepare, *[lambda *done: done] * (len(halvings(cells)) - 4), send, receive]
    weights, done = gather_cells(master.astype(BF16), cells, steps, start)
    (embedded, normed, normed_t, ghosts), held, *halves = done

    columns = heads * atoms
    energies, grads = pl.pallas_call(
        sweep_kernel,
        out_shape=(struct((1, atoms), F32), struct((4, width, width), F32)),
        in_specs=vmem(11),
        out_specs=tuple(vmem(2)),
        scratch_shapes=[
            pltpu.VMEM((table_rows, columns), F32),
            pltpu.VMEM((table_rows, columns), F32),
            pltpu.VMEM((table_rows, columns), BF16),
            pltpu.VMEM((table_rows, columns), BF16),
        ],
        compiler_params=pltpu.CompilerParams(vmem_limit_bytes=32 * 1024 * 1024),
        name="sweep",
    )(weights, normed, normed_t, ghosts, embedded, *halves[0], *halves[1], *held)

    parts = grads.reshape(4, cells, width // cells, width).transpose(1, 0, 2, 3)
    owned = reduce_all(parts, cells, bricks)
    moment_new = 0.9 * moment + 0.1 * owned
    second_new = 0.999 * second + 0.001 * owned * owned
    adam_step = moment_new / (jnp.sqrt(second_new) + 1e-08)
    return (energies[None], moment_new, second_new, adam_step)


def solution(mesh):
    return jax.shard_map(
        functools.partial(body, mesh.shape["cell"], mesh.shape["brick"]),
        mesh=mesh,
        in_specs=(
            P("cell", "brick", None, None),
            P("cell", "brick", None),
            P(),
            P("cell", "brick", None, None),
            P("cell", "brick", None),
            P("cell", "brick", None, None),
            P("cell", "brick", None, None),
            P(),
            P(),
            P(),
            P("cell", "brick", None),
            P(None, "cell", None),
            P(None, "cell", None),
            P(None, "cell", None),
        ),
        out_specs=(
            P("cell", "brick", None),
            P(None, "cell", None),
            P(None, "cell", None),
            P(None, "cell", None),
        ),
        check_vma=False,
    )
```

```python
import functools
import math

import jax
import jax.numpy as jnp
from jax import lax
from jax.experimental import pallas as pl
from jax.experimental.pallas import tpu as pltpu
from jax.sharding import PartitionSpec as P

CHUNK = 32
DEPTH = 5
FAR = 1e30
FAR_ROW = 1 << 20
PACK_ROWS = 16

loss_weight = 0.0625
epsilon_norm = 1e-06

F32 = jnp.float32
BF16 = jnp.bfloat16
NT = (((1,), (1,)), ((), ()))
TN = (((0,), (0,)), ((), ()))


def dot(a, b):
    return jnp.dot(a, b, preferred_element_type=F32)


def dot_nt(a, b):
    return lax.dot_general(a, b, NT, preferred_element_type=F32)


def dot_tn(a, b):
    return lax.dot_general(a, b, TN, preferred_element_type=F32)


def to_column(row):
    n = row.shape[1]
    eye = lax.broadcasted_iota(jnp.int32, (n, n), 0) == lax.broadcasted_iota(jnp.int32, (n, n), 1)
    return jnp.sum(jnp.where(eye, row, jnp.zeros_like(row)), axis=1, keepdims=True)


def to_row(column):
    n = column.shape[0]
    eye = lax.broadcasted_iota(jnp.int32, (n, n), 0) == lax.broadcasted_iota(jnp.int32, (n, n), 1)
    return jnp.sum(jnp.where(eye, column, jnp.zeros_like(column)), axis=0, keepdims=True)


def embed(features, species, species_table, norm_gain, send_rows, embedded, normed, normed_t, parcel):
    atoms = features.shape[0]
    column = to_column(species)
    picked = jnp.zeros_like(features)
    for kind in range(species_table.shape[0]):
        row = species_table[kind : kind + 1, :].astype(F32)
        picked = jnp.where(column == kind, row, picked)
    total = features + picked
    embedded[...] = total
    scale = lax.rsqrt(jnp.mean(total * total, axis=-1, keepdims=True) + epsilon_norm)
    norm = total * scale * norm_gain[...]
    half = norm.astype(BF16)
    normed[...] = half
    normed_t[...] = norm.T.astype(BF16)
    bricks, slots = send_rows.shape
    for brick in range(bricks):
        chosen = send_rows[brick : brick + 1, :]
        picks = (lax.broadcasted_iota(jnp.int32, (atoms, slots), 0) == chosen).astype(F32).astype(BF16)
        parcel[brick] = dot_tn(picks, half).astype(BF16)


def terms_of(value):
    high = value.astype(BF16).astype(F32)
    rest = value - high
    middle = rest.astype(BF16).astype(F32)
    return [high, middle, rest - middle]


def embed_kernel(pack, master, features, species, send_rows, species_table, norm_gain, *refs):
    count = (len(refs) - 5 - pack) // 2
    sources, (shard, embedded, normed, normed_t, parcel) = refs[:count], refs[count : count + 5]
    kept = refs[count + 5 :]
    shard[...] = master[...].astype(BF16)
    for source, target in zip(sources, kept):
        target[...] = source[...]
    if pack:
        neighbours, counts, distances, targets = sources[:4]
        packed = kept[-1]
        slots, atoms = neighbours.shape
        width = features.shape[1]
        arrays = [features[:, at : at + atoms].astype(F32) for at in range(0, width, atoms)]
        arrays += [neighbours[...].astype(F32), *terms_of(distances[...])]
        bricks, sent = send_rows.shape
        rows = [species[...].astype(F32), counts[...].astype(F32), *terms_of(targets[...])]
        lists = jnp.concatenate([send_rows[...].astype(F32), jnp.zeros((bricks, atoms - sent), F32)], axis=1)
        rows += [lists, jnp.zeros((PACK_ROWS - len(rows) - bricks, atoms), F32)]
        start = 0
        for array in [*arrays, jnp.concatenate(rows, axis=0)]:
            packed[start : start + array.shape[0], :] = array.astype(BF16)
            start += array.shape[0]
    embed(features[...].astype(F32), species[...], species_table, norm_gain, send_rows, embedded, normed, normed_t, parcel)


def unpack_kernel(packed, species_table, norm_gain, embedded, normed, normed_t, parcel, neighbours, counts, distances, targets):
    slots, atoms = neighbours.shape
    width = embedded.shape[1]
    bricks, sent = parcel.shape[:2]
    start = 0

    def take(rows):
        nonlocal start
        start += rows
        return packed[start - rows : start, :].astype(F32)

    features = jnp.concatenate([take(atoms) for _ in range(width // atoms)], axis=1)
    neighbours[...] = take(slots).astype(jnp.int32)
    distances[...] = take(slots) + take(slots) + take(slots)
    rows = take(PACK_ROWS)
    counts[...] = rows[1:2].astype(jnp.int32)
    targets[...] = rows[2:3] + rows[3:4] + rows[4:5]
    send_rows = rows[5 : 5 + bricks, :sent].astype(jnp.int32)
    species = rows[0:1].astype(jnp.int32)
    embed(features, species, species_table, norm_gain, send_rows, embedded, normed, normed_t, parcel)


def index_kernel(first, neighbours, counts, distances, decay, weight, absent, key_ref):
    slots, atoms = neighbours.shape
    heads, table_rows = weight.shape[:2]
    slot = lax.broadcasted_iota(jnp.int32, (slots, atoms), 0)
    valid = slot < counts[...]
    held = jnp.where(valid, neighbours[...] - first, -FAR_ROW - slot)
    key_ref[...] = held
    slope = [-decay[:, h : h + 1] for h in range(heads)]

    def chunk(step, nearest):
        start = pl.multiple_of(step * CHUNK, CHUNK)
        at = pl.ds(start, CHUNK)
        row = lax.broadcasted_iota(jnp.int32, (CHUNK, atoms), 0) + start
        layers = [jnp.full((CHUNK, atoms), FAR, F32) for _ in range(DEPTH)]
        for j in range(slots):
            hit = row == key_ref[j : j + 1, :]
            entering = distances[j : j + 1, :]
            for k in range(DEPTH):
                entering, layers[k] = layers[k], jnp.where(hit, entering, layers[k])
        absent[at, :] = jnp.where(layers[0] < FAR, 0.0, -FAR)
        for h in range(heads):
            weight[h, at, :] = sum(jnp.exp(slope[h] * layer) for layer in layers)
        return jnp.minimum(nearest, jnp.min(layers[-1], axis=0, keepdims=True))

    nearest = lax.fori_loop(0, table_rows // CHUNK, chunk, jnp.full((1, atoms), FAR, F32))

    @pl.when(jnp.min(nearest) < FAR)
    def _():
        rank = jnp.zeros((slots, atoms), jnp.int32)
        for j in range(slots):
            rank += ((held == key_ref[j : j + 1, :]) & (slot < j)).astype(jnp.int32)
        inside = valid & (held >= 0) & (held < table_rows)
        key_ref[...] = jnp.where(inside, held + table_rows * rank, -1)

        def layer(level, carry):
            for start in range(0, table_rows, CHUNK):
                at = pl.ds(start, CHUNK)
                row = lax.broadcasted_iota(jnp.int32, (CHUNK, atoms), 0) + (start + level * table_rows)
                distance = jnp.full((CHUNK, atoms), FAR, F32)
                for j in range(slots):
                    distance = jnp.where(row == key_ref[j : j + 1, :], distances[j : j + 1, :], distance)
                for h in range(heads):
                    weight[h, at, :] += jnp.exp(slope[h] * distance)
            return carry

        lax.fori_loop(DEPTH, jnp.max(rank) + 1, layer, 0)


def sweep_kernel(count, weights, readout, *refs):
    operands, scratch = 9, 4
    energies, grads = refs[operands * count : operands * count + 2]
    bricks = [refs[operands * i : operands * (i + 1)] for i in range(count)]
    start = operands * count + 2
    memory = [refs[start + scratch * i : start + scratch * (i + 1)] for i in range(count)]
    atoms, width = bricks[0][0].shape
    heads = bricks[0][4].shape[0]
    head_size = width // heads
    scale = 1.0 / math.sqrt(head_size)
    head_of = lax.broadcasted_iota(jnp.int32, (atoms, width), 1) // head_size
    group = math.gcd(heads, 4)
    out_proj = weights[3]

    def stacked(array):
        zero = jnp.zeros_like(array)
        return jnp.concatenate([jnp.where(head_of == h, array, zero) for h in range(heads)], axis=0)

    def own_channels(turned, blocks):
        parts = []
        for h in range(0, heads, group):
            channels = turned[h * head_size : (h + group) * head_size]
            wide = dot(channels, blocks[:, h * atoms : (h + group) * atoms])
            for i in range(group):
                parts.append(wide[i * head_size : (i + 1) * head_size, i * atoms : (i + 1) * atoms])
        return jnp.concatenate(parts, axis=0)

    def forward(i):
        normed, normed_t, ghosts, embedded, weight, absent, weight_rest, absent_rest, targets = bricks[i]
        score_ref, att_ref, att_half, _ = memory[i]
        norm = normed[...]
        table = jnp.concatenate([norm, ghosts[...]], axis=0)
        table_t = jnp.concatenate([normed_t[...], ghosts[...].astype(F32).T.astype(BF16)], axis=1)
        query = stacked(dot(norm, weights[0]).astype(BF16))
        keys = dot(table, weights[1])
        values = dot(table, weights[2])
        keys_t, values_t = keys.T.astype(BF16), values.T.astype(BF16)
        keys, values = keys.astype(BF16), values.astype(BF16)
        score_ref[...] = dot_nt(keys, query)
        gone = jnp.concatenate([absent[...], absent_rest[...]], axis=0)
        for h in range(heads):
            at = pl.ds(h * atoms, atoms)
            score = score_ref[:, at] + gone
            weights_h = jnp.concatenate([weight[h], weight_rest[h]], axis=0)
            score = (score - jnp.max(score, axis=0, keepdims=True)) * (scale * math.log2(math.e))
            terms = jnp.exp2(score) * weights_h
            attention = terms * (1.0 / jnp.sum(terms, axis=0, keepdims=True))
            att_ref[:, at] = attention
            att_half[:, at] = attention.astype(BF16)
        return table_t, query, keys_t, values, own_channels(values_t, att_half[...])

    def middle(i, attended_t):
        embedded, targets = bricks[i][3], bricks[i][8]
        updated = embedded[...] + dot(attended_t.T.astype(BF16), out_proj)
        sigmoid = 1.0 / (1.0 + jnp.exp(-updated))
        energy = jnp.sum(readout[...] * (updated * sigmoid), axis=1, keepdims=True)
        if i == 0:
            energies[...] = to_row(energy)
        grad_energy = loss_weight * (energy - to_column(targets[...]))
        slope = sigmoid * (1.0 + updated * (1.0 - sigmoid))
        grad_updated = (grad_energy * readout[...] * slope).astype(BF16)
        grad_out = dot(attended_t.astype(BF16), grad_updated)
        return grad_out, stacked(dot_nt(grad_updated, out_proj).astype(BF16))

    def backward(i, table_t, query, keys_t, values, grad_attended):
        normed_t = bricks[i][1]
        score_ref, att_ref, att_half, grad_score = memory[i]
        score_ref[...] = dot_nt(values, grad_attended)
        for h in range(heads):
            at = pl.ds(h * atoms, atoms)
            attention = att_ref[:, at]
            grad_weights = score_ref[:, at]
            mean = jnp.sum(attention * grad_weights, axis=0, keepdims=True)
            grad_score[:, at] = (attention * (grad_weights - mean)).astype(BF16)
        value_grads = dot(att_half[...], grad_attended)
        grad_value = dot(table_t, value_grads.astype(BF16))
        grad_query_t = own_channels(keys_t, grad_score[...]) * scale
        grad_query = dot_nt(normed_t[...], grad_query_t.astype(BF16))
        key_grads = dot(grad_score[...], query) * scale
        return grad_query, dot(table_t, key_grads.astype(BF16)), grad_value

    first = [forward(i) for i in range(count)]
    second = [middle(i, first[i][4]) for i in range(count)]
    third = [backward(i, *first[i][:4], second[i][1]) for i in range(count)]
    for place in range(3):
        grads[place] = sum(third[i][place] for i in range(1, count)) + third[0][place]
    grads[3] = sum(second[i][0] for i in range(1, count)) + second[0][0]


def vmem(count):
    return [pl.BlockSpec(memory_space=pltpu.VMEM)] * count


SMEM = pl.BlockSpec(memory_space=pltpu.SMEM)


def struct(shape, dtype):
    return jax.ShapeDtypeStruct(shape, dtype)


def pinned(shape, dtype):
    return pltpu.VMEM(shape, dtype)


def halvings(size):
    offsets = []
    offset = size // 2
    while offset:
        offsets.append(offset)
        offset //= 2
    return offsets


def crossing(offset, crossed):
    return offset | 1 if offset in crossed else offset


def own_core(cells, crossed):
    place = lax.axis_index("cell")
    blocks = 2 * jnp.arange(cells // 2)
    core = jnp.full((cells // 2,), place % 2)
    for offset in crossed:
        core = core ^ ((blocks // offset) % 2) ^ ((place // offset) % 2)
    return core


def swap(array, cells, vector_of):
    return lax.ppermute(array, "cell", [(i, i ^ vector_of(i)) for i in range(cells)])


def gather_cells(shard, cells, beside):
    place = lax.axis_index("cell")
    offsets = halvings(cells)[:-1]
    far, (a, b) = offsets[:-2], offsets[-2:]
    crossed = [*far, b]
    held = shard
    done = ()

    def step(vectors):
        nonlocal done
        work = beside.pop(0)(*done) if beside else done
        arrived = [swap(held, cells, lambda i, vector=vector: vector) for vector in vectors]
        done, arrived = lax.optimization_barrier((work, arrived))
        return arrived

    def placed(first, second, offset):
        own = (place // offset) % 2 == 0
        return jnp.where(own, jnp.stack([first, second]), jnp.stack([second, first]))

    for offset in far:
        held = placed(held, step([crossing(offset, crossed)])[0], offset)
    vectors = [crossing(offset, crossed) for offset in (a, b)]
    over_both, over_a, over_b = step([vectors[0] ^ vectors[1], *vectors])
    held = placed(placed(held, over_b, b), placed(over_a, over_both, b), a)
    (arrived,) = step([1])
    count = len(offsets)
    order = (*reversed(range(2, count)), 0, 1, *range(count, held.ndim))
    held, arrived = held.transpose(order), arrived.transpose(order)
    core = own_core(cells, crossed).reshape((2,) * count + (1,) * shard.ndim)
    pair = [jnp.where(core == 0, held, arrived), jnp.where(core == 0, arrived, held)]
    blocks = jnp.stack(pair, axis=count).reshape((cells,) + shard.shape)
    return blocks.transpose(1, 0, 2, 3).reshape(shard.shape[0], -1, shard.shape[2]), done


def reduce_all(parts, cells, bricks, across):
    place = lax.axis_index("cell")
    tail = parts.shape[1:]
    left = halvings(cells)[:-1]
    near, middle, farthest = left[-2:], left[1:-2], left[0]
    crossed = [near[0], *middle, farthest]
    parts = parts.reshape((cells // 2, 2) + tail)
    core = own_core(cells, crossed).reshape((cells // 2,) + (1,) * len(tail))
    keep = jnp.where(core == 0, parts[:, 0], parts[:, 1])
    send = jnp.where(core == 0, parts[:, 1], parts[:, 0])
    total = keep + swap(send.astype(BF16), cells, lambda i: 1).astype(F32)
    total = total.reshape((2,) * len(left) + tail)

    def portion(array, flipped):
        for offset, flip in reversed(flipped):
            bit = (place // offset) % 2
            array = lax.dynamic_index_in_dim(array, 1 - bit if flip else bit, left.index(offset), False)
        return array

    def exchange(group):
        nonlocal total, left
        mine = portion(total, [(offset, 0) for offset in group])
        for step in range(1, 1 << len(group)):
            flipped = [(offset, step >> k & 1) for k, offset in enumerate(group)]
            vector = 0
            for offset, flip in flipped:
                vector ^= crossing(offset, crossed) * flip
            sent = portion(total, flipped).astype(BF16)
            mine = mine + swap(sent, cells, lambda i, vector=vector: vector).astype(F32)
        total = mine
        left = [offset for offset in left if offset not in group]

    exchange(near)
    for offset in reversed(middle):
        exchange([offset])

    def meet(array, vector, step):
        pairs = [
            (cell * bricks + brick, (cell ^ vector) * bricks + (brick ^ step))
            for cell in range(cells)
            for brick in range(bricks)
        ]
        return lax.ppermute(array, ("cell", "brick"), pairs).astype(F32)

    vector = crossing(farthest, crossed)
    keep = portion(total, [(farthest, 0)])
    send = portion(total, [(farthest, 1)]).astype(BF16)
    if across:
        keep = keep.astype(BF16)
    total = keep.astype(F32) + meet(send, vector, 0)
    if across:
        far = meet(send, vector, across[0])
        total = total + (far + meet(keep, 0, across[0]))
    for step in across[1:]:
        keep = total.astype(BF16)
        total = keep.astype(F32) + meet(keep, 0, step)
    return total


def body(
    cells,
    bricks,
    features,
    species,
    species_table,
    neighbours,
    counts,
    send_lists,
    distances,
    head_decay,
    norm_gain,
    readout,
    targets,
    master,
    moment,
    second,
):
    atoms, width = features.shape[2:]
    slots = neighbours.shape[2]
    ghost_slots = send_lists.shape[3]
    heads = head_decay.shape[0]
    table_rows = atoms + bricks * ghost_slots

    paired = bricks == 2 and table_rows <= 256
    count = 2 if paired else 1
    brick = lax.axis_index("brick")
    part = table_rows // 2
    own = (features[0, 0], species[0], send_lists[0, 0])
    slot_arrays = (neighbours[0, 0], counts[0], distances[0, 0], targets[0])
    common = (species_table, norm_gain[None])
    embed_shapes = (
        pinned((atoms, width), F32),
        pinned((atoms, width), BF16),
        pinned((width, atoms), BF16),
        pinned((bricks, ghost_slots, width), BF16),
    )
    slot_shapes = tuple(pinned(array.shape, array.dtype) for array in slot_arrays)
    small = pltpu.CompilerParams(vmem_limit_bytes=8 * 1024 * 1024)

    def embed_own():
        rest = (head_decay[None], readout[None], *common)
        shapes = (pinned(master.shape, BF16),) + embed_shapes + slot_shapes
        shapes += tuple(pinned(array.shape, array.dtype) for array in rest)
        if paired:
            shapes += (pinned((width + 4 * slots + PACK_ROWS, atoms), BF16),)
        outs = pl.pallas_call(
            functools.partial(embed_kernel, int(paired)),
            out_shape=shapes,
            in_specs=vmem(6 + len(slot_arrays) + len(rest)),
            out_specs=tuple(vmem(len(shapes))),
            name="embed",
        )(master, *own, *common, *slot_arrays, *rest)
        return outs[0], outs[1:5], outs[5:9], outs[9:13], outs[13:]

    def embed_partner(packed, *common):
        outs = pl.pallas_call(
            unpack_kernel,
            out_shape=embed_shapes + slot_shapes,
            in_specs=vmem(3),
            out_specs=tuple(vmem(8)),
            compiler_params=small,
            name="unpack",
        )(packed, *common)
        return outs[:4], outs[4:]

    def index(first, arrays, decay):
        return pl.pallas_call(
            functools.partial(index_kernel, first),
            out_shape=(pinned((heads, part, atoms), F32), pinned((part, atoms), F32)),
            in_specs=vmem(4),
            out_specs=tuple(vmem(2)),
            scratch_shapes=[pltpu.VMEM((slots, atoms), jnp.int32)],
            compiler_params=small,
            name="index",
        )(*arrays[:3], decay)

    def over_bricks(array, offset):
        return lax.ppermute(array, "brick", [(i, i ^ offset) for i in range(bricks)])

    def ghosts_from(parcel):
        ghosts = parcel
        for offset in range(1, bricks):
            peer = brick ^ offset
            arrived = over_bricks(lax.dynamic_index_in_dim(parcel, peer, 0, True), offset)
            ghosts = lax.dynamic_update_slice_in_dim(ghosts, arrived, peer, 0)
        return ghosts.reshape(bricks * ghost_slots, width)

    def ghosts_of(parcels, place):
        chosen = [lax.dynamic_index_in_dim(parcel, place, 0, False) for parcel in parcels]
        ordered = jnp.where(brick == 0, jnp.stack(chosen), jnp.stack(chosen[::-1]))
        return ordered.reshape(bricks * ghost_slots, width)

    late = []

    shard, state, arrays, (decay, gain, *kept), packed = embed_own()

    def prepare():
        if paired:
            late.extend([over_bricks(packed[0], 1), *kept])
        return state, arrays, decay, gain, index(0, arrays, decay)

    def gather_ghosts(state, arrays, decay, gain, half):
        rows = ghosts_from(state[3])
        return [(state, rows, arrays[3], half, index(part, arrays, decay))], gain

    def visit_partner(state, arrays, decay, gain, half):
        rest = index(part, arrays, decay)
        partner, partner_arrays = embed_partner(*late)
        partner_half = index(0, partner_arrays, decay)
        return (state, arrays[3], half, rest), (partner, partner_arrays, partner_half), decay, gain

    def finish_partner(mine, other, decay, gain):
        state, wanted, half, rest = mine
        partner, arrays, partner_half = other
        parcels = (state[3], partner[3])
        return [
            (state, ghosts_of(parcels, brick), wanted, half, rest),
            (partner, ghosts_of(parcels, 1 - brick), arrays[3], partner_half, index(part, arrays, decay)),
        ], gain

    steps = [prepare, *[lambda *done: done] * (len(halvings(cells)) - 4)]
    steps += [visit_partner, finish_partner] if paired else [gather_ghosts]
    weights, (worked, gain) = gather_cells(shard, cells, steps)
    operands = []
    for (embedded, normed, normed_t, _), ghosts, wanted, half, rest in worked:
        operands += [normed, normed_t, ghosts, embedded, *half, *rest, wanted]

    columns = heads * atoms
    energies, grads = pl.pallas_call(
        functools.partial(sweep_kernel, count),
        out_shape=(struct((1, atoms), F32), struct((4, width, width), F32)),
        in_specs=vmem(2 + len(operands)),
        out_specs=tuple(vmem(2)),
        scratch_shapes=[
            pltpu.VMEM((table_rows, columns), F32),
            pltpu.VMEM((table_rows, columns), F32),
            pltpu.VMEM((table_rows, columns), BF16),
            pltpu.VMEM((table_rows, columns), BF16),
        ]
        * count,
        compiler_params=pltpu.CompilerParams(vmem_limit_bytes=32 * 1024 * 1024),
        name="sweep",
    )(weights, gain, *operands)

    parts = grads.reshape(4, cells, width // cells, width).transpose(1, 0, 2, 3)
    across = [] if paired else list(reversed(halvings(bricks)))
    owned = reduce_all(parts, cells, bricks, across)
    moment_new = 0.9 * moment + 0.1 * owned
    second_new = 0.999 * second + 0.001 * owned * owned
    adam_step = moment_new / (jnp.sqrt(second_new) + 1e-08)
    return (energies[None], moment_new, second_new, adam_step)


def solution(mesh):
    return jax.shard_map(
        functools.partial(body, mesh.shape["cell"], mesh.shape["brick"]),
        mesh=mesh,
        in_specs=(
            P("cell", "brick", None, None),
            P("cell", "brick", None),
            P(),
            P("cell", "brick", None, None),
            P("cell", "brick", None),
            P("cell", "brick", None, None),
            P("cell", "brick", None, None),
            P(),
            P(),
            P(),
            P("cell", "brick", None),
            P(None, "cell", None),
            P(None, "cell", None),
            P(None, "cell", None),
        ),
        out_specs=(
            P("cell", "brick", None),
            P(None, "cell", None),
            P(None, "cell", None),
            P(None, "cell", None),
        ),
        check_vma=False,
    )
```

```python
import functools
import math

import jax
import jax.numpy as jnp
from jax import lax
from jax.experimental import pallas as pl
from jax.experimental.pallas import tpu as pltpu
from jax.sharding import PartitionSpec as P

CHUNK = 32
DEPTH = 5
FAR = 1e30
FAR_ROW = 1 << 20
PACK_ROWS = 16

loss_weight = 0.0625
epsilon_norm = 1e-06

F32 = jnp.float32
BF16 = jnp.bfloat16
NT = (((1,), (1,)), ((), ()))
TN = (((0,), (0,)), ((), ()))


def dot(a, b):
    return jnp.dot(a, b, preferred_element_type=F32)


def dot_nt(a, b):
    return lax.dot_general(a, b, NT, preferred_element_type=F32)


def dot_tn(a, b):
    return lax.dot_general(a, b, TN, preferred_element_type=F32)


def to_column(row):
    n = row.shape[1]
    eye = lax.broadcasted_iota(jnp.int32, (n, n), 0) == lax.broadcasted_iota(jnp.int32, (n, n), 1)
    return jnp.sum(jnp.where(eye, row, jnp.zeros_like(row)), axis=1, keepdims=True)


def to_row(column):
    n = column.shape[0]
    eye = lax.broadcasted_iota(jnp.int32, (n, n), 0) == lax.broadcasted_iota(jnp.int32, (n, n), 1)
    return jnp.sum(jnp.where(eye, column, jnp.zeros_like(column)), axis=0, keepdims=True)


def embed(features, species, species_table, norm_gain, send_rows, embedded, normed, normed_t, parcel):
    atoms = features.shape[0]
    column = to_column(species)
    picked = jnp.zeros_like(features)
    for kind in range(species_table.shape[0]):
        row = species_table[kind : kind + 1, :].astype(F32)
        picked = jnp.where(column == kind, row, picked)
    total = features + picked
    embedded[...] = total
    scale = lax.rsqrt(jnp.mean(total * total, axis=-1, keepdims=True) + epsilon_norm)
    norm = total * scale * norm_gain[...]
    half = norm.astype(BF16)
    normed[...] = half
    normed_t[...] = norm.T.astype(BF16)
    bricks, slots = send_rows.shape
    for brick in range(bricks):
        chosen = send_rows[brick : brick + 1, :]
        picks = (lax.broadcasted_iota(jnp.int32, (atoms, slots), 0) == chosen).astype(F32).astype(BF16)
        parcel[brick] = dot_tn(picks, half).astype(BF16)


def terms_of(value):
    high = value.astype(BF16).astype(F32)
    rest = value - high
    middle = rest.astype(BF16).astype(F32)
    return [high, middle, rest - middle]


def embed_kernel(pack, master, features, species, send_rows, species_table, norm_gain, *refs):
    count = (len(refs) - 5 - pack) // 2
    sources, (shard, embedded, normed, normed_t, parcel) = refs[:count], refs[count : count + 5]
    kept = refs[count + 5 :]
    shard[...] = master[...].astype(BF16)
    for source, target in zip(sources, kept):
        target[...] = source[...]
    if pack:
        neighbours, counts, distances, targets = sources[:4]
        packed = kept[-1]
        slots, atoms = neighbours.shape
        width = features.shape[1]
        arrays = [features[:, at : at + atoms].astype(F32) for at in range(0, width, atoms)]
        arrays += [neighbours[...].astype(F32), *terms_of(distances[...])]
        bricks, sent = send_rows.shape
        rows = [species[...].astype(F32), counts[...].astype(F32), *terms_of(targets[...])]
        lists = jnp.concatenate([send_rows[...].astype(F32), jnp.zeros((bricks, atoms - sent), F32)], axis=1)
        rows += [lists, jnp.zeros((PACK_ROWS - len(rows) - bricks, atoms), F32)]
        start = 0
        for array in [*arrays, jnp.concatenate(rows, axis=0)]:
            packed[start : start + array.shape[0], :] = array.astype(BF16)
            start += array.shape[0]
    embed(features[...].astype(F32), species[...], species_table, norm_gain, send_rows, embedded, normed, normed_t, parcel)


def unpack_kernel(packed, species_table, norm_gain, embedded, normed, normed_t, parcel, neighbours, counts, distances, targets):
    slots, atoms = neighbours.shape
    width = embedded.shape[1]
    bricks, sent = parcel.shape[:2]
    start = 0

    def take(rows):
        nonlocal start
        start += rows
        return packed[start - rows : start, :].astype(F32)

    features = jnp.concatenate([take(atoms) for _ in range(width // atoms)], axis=1)
    neighbours[...] = take(slots).astype(jnp.int32)
    distances[...] = take(slots) + take(slots) + take(slots)
    rows = take(PACK_ROWS)
    counts[...] = rows[1:2].astype(jnp.int32)
    targets[...] = rows[2:3] + rows[3:4] + rows[4:5]
    send_rows = rows[5 : 5 + bricks, :sent].astype(jnp.int32)
    species = rows[0:1].astype(jnp.int32)
    embed(features, species, species_table, norm_gain, send_rows, embedded, normed, normed_t, parcel)


def index_kernel(first, neighbours, counts, distances, decay, weight, absent, key_ref):
    slots, atoms = neighbours.shape
    heads, table_rows = weight.shape[:2]
    slot = lax.broadcasted_iota(jnp.int32, (slots, atoms), 0)
    valid = slot < counts[...]
    held = jnp.where(valid, neighbours[...] - first, -FAR_ROW - slot)
    key_ref[...] = held
    slope = [-decay[:, h : h + 1] for h in range(heads)]

    def chunk(step, nearest):
        start = pl.multiple_of(step * CHUNK, CHUNK)
        at = pl.ds(start, CHUNK)
        row = lax.broadcasted_iota(jnp.int32, (CHUNK, atoms), 0) + start
        layers = [jnp.full((CHUNK, atoms), FAR, F32) for _ in range(DEPTH)]
        for j in range(slots):
            hit = row == key_ref[j : j + 1, :]
            entering = distances[j : j + 1, :]
            for k in range(DEPTH):
                entering, layers[k] = layers[k], jnp.where(hit, entering, layers[k])
        absent[at, :] = jnp.where(layers[0] < FAR, 0.0, -FAR)
        for h in range(heads):
            weight[h, at, :] = sum(jnp.exp(slope[h] * layer) for layer in layers)
        return jnp.minimum(nearest, jnp.min(layers[-1], axis=0, keepdims=True))

    nearest = lax.fori_loop(0, table_rows // CHUNK, chunk, jnp.full((1, atoms), FAR, F32))

    @pl.when(jnp.min(nearest) < FAR)
    def _():
        rank = jnp.zeros((slots, atoms), jnp.int32)
        for j in range(slots):
            rank += ((held == key_ref[j : j + 1, :]) & (slot < j)).astype(jnp.int32)
        inside = valid & (held >= 0) & (held < table_rows)
        key_ref[...] = jnp.where(inside, held + table_rows * rank, -1)

        def layer(level, carry):
            for start in range(0, table_rows, CHUNK):
                at = pl.ds(start, CHUNK)
                row = lax.broadcasted_iota(jnp.int32, (CHUNK, atoms), 0) + (start + level * table_rows)
                distance = jnp.full((CHUNK, atoms), FAR, F32)
                for j in range(slots):
                    distance = jnp.where(row == key_ref[j : j + 1, :], distances[j : j + 1, :], distance)
                for h in range(heads):
                    weight[h, at, :] += jnp.exp(slope[h] * distance)
            return carry

        lax.fori_loop(DEPTH, jnp.max(rank) + 1, layer, 0)


def sweep_kernel(count, cells, held, arrived, readout, *refs):
    operands, scratch = 9, 4
    energies, keep, send = refs[operands * count : operands * count + 3]
    bricks = [refs[operands * i : operands * (i + 1)] for i in range(count)]
    start = operands * count + 3
    weights = refs[-1]
    assemble(held, arrived, weights, cells)
    memory = [refs[start + scratch * i : start + scratch * (i + 1)] for i in range(count)]
    atoms, width = bricks[0][0].shape
    heads = bricks[0][4].shape[0]
    head_size = width // heads
    scale = 1.0 / math.sqrt(head_size)
    head_of = lax.broadcasted_iota(jnp.int32, (atoms, width), 1) // head_size
    group = math.gcd(heads, 2)
    out_proj = weights[3]

    def stacked(array):
        zero = jnp.zeros_like(array)
        return jnp.concatenate([jnp.where(head_of == h, array, zero) for h in range(heads)], axis=0)

    def own_channels(turned, blocks, h):
        channels = turned[h * head_size : (h + group) * head_size]
        wide = dot(channels, blocks[:, h * atoms : (h + group) * atoms])
        return [wide[i * head_size : (i + 1) * head_size, i * atoms : (i + 1) * atoms] for i in range(group)]

    def work(i):
        normed, normed_t, ghosts, embedded, weight, absent, weight_rest, absent_rest, targets = bricks[i]
        score_ref, att_ref, att_half, grad_score = memory[i]
        norm = normed[...]
        table = jnp.concatenate([norm, ghosts[...]], axis=0)
        query = stacked(dot(norm, weights[0]).astype(BF16))
        keys = dot(table, weights[1])
        values = dot(table, weights[2])
        yield
        keys_t, values_t = keys.T.astype(BF16), values.T.astype(BF16)
        keys, values = keys.astype(BF16), values.astype(BF16)
        score_ref[...] = dot_nt(keys, query)
        yield
        gone = jnp.concatenate([absent[...], absent_rest[...]], axis=0)
        parts = []
        for h in range(heads):
            at = pl.ds(h * atoms, atoms)
            score = score_ref[:, at] + gone
            weights_h = jnp.concatenate([weight[h], weight_rest[h]], axis=0)
            score = (score - jnp.max(score, axis=0, keepdims=True)) * (scale * math.log2(math.e))
            terms = jnp.exp2(score) * weights_h
            attention = terms * (1.0 / jnp.sum(terms, axis=0, keepdims=True))
            att_ref[:, at] = attention
            att_half[:, at] = attention.astype(BF16)
            if h % group == group - 1:
                parts += own_channels(values_t, att_half, h - group + 1)
        attended_t = jnp.concatenate(parts, axis=0)
        yield
        updated = embedded[...] + dot(attended_t.T.astype(BF16), out_proj)
        sigmoid = 1.0 / (1.0 + jnp.exp(-updated))
        energy = jnp.sum(readout[...] * (updated * sigmoid), axis=1, keepdims=True)
        if i == 0:
            energies[...] = to_row(energy)
        grad_energy = loss_weight * (energy - to_column(targets[...]))
        slope = sigmoid * (1.0 + updated * (1.0 - sigmoid))
        grad_updated = (grad_energy * readout[...] * slope).astype(BF16)
        yield
        grad_out = dot(attended_t.astype(BF16), grad_updated)
        grad_attended = stacked(dot_nt(grad_updated, out_proj).astype(BF16))
        yield
        score_ref[...] = dot_nt(values, grad_attended)
        yield
        table_t = jnp.concatenate([normed_t[...], ghosts[...].astype(F32).T.astype(BF16)], axis=1)
        value_grads = dot(att_half[...], grad_attended)
        grad_value = dot(table_t, value_grads.astype(BF16))
        yield
        parts = []
        for h in range(heads):
            at = pl.ds(h * atoms, atoms)
            attention = att_ref[:, at]
            grad_weights = score_ref[:, at]
            mean = jnp.sum(attention * grad_weights, axis=0, keepdims=True)
            grad_score[:, at] = (attention * (grad_weights - mean)).astype(BF16)
            if h % group == group - 1:
                parts += own_channels(keys_t, grad_score, h - group + 1)
        yield
        key_grads = dot(grad_score[...], query) * scale
        yield
        grad_query_t = jnp.concatenate(parts, axis=0) * scale
        grad_query = dot_nt(normed_t[...], grad_query_t.astype(BF16))
        yield grad_query, dot(table_t, key_grads.astype(BF16)), grad_value, grad_out

    running = [work(i) for i in range(count)]
    found = [None] * count
    while found[0] is None:
        found = [next(step) for step in running]
    crossed = reduce_groups(cells)[3]
    place = lax.axis_index("cell")
    core = place % 2
    for offset in crossed:
        core = core ^ ((place // offset) % 2)
    for matrix in range(4):
        total = sum(part[matrix] for part in found[1:]) + found[0][matrix]
        blocks = total.reshape((cells // 2, 2) + keep.shape[2:])
        for k in range(cells // 2):
            first = core == sum(2 * k // offset for offset in crossed) % 2
            keep[k, matrix] = jnp.where(first, blocks[k, 0], blocks[k, 1])
            send[k, matrix] = jnp.where(first, blocks[k, 1], blocks[k, 0]).astype(BF16)


def vmem(count):
    return [pl.BlockSpec(memory_space=pltpu.VMEM)] * count


SMEM = pl.BlockSpec(memory_space=pltpu.SMEM)


def struct(shape, dtype):
    return jax.ShapeDtypeStruct(shape, dtype)


def pinned(shape, dtype):
    return pltpu.VMEM(shape, dtype)


def halvings(size):
    offsets = []
    offset = size // 2
    while offset:
        offsets.append(offset)
        offset //= 2
    return offsets


def crossing(offset, crossed):
    return offset | 1 if offset in crossed else offset


def swap(array, cells, vector_of):
    return lax.ppermute(array, "cell", [(i, i ^ vector_of(i)) for i in range(cells)])


def gather_cells(shard, cells, beside):
    place = lax.axis_index("cell")
    offsets = halvings(cells)[:-1]
    far, (a, b) = offsets[:-2], offsets[-2:]
    crossed = [*far, b]
    held = shard
    done = ()

    def step(vectors):
        nonlocal done
        work = beside.pop(0)(*done) if beside else done
        arrived = [swap(held, cells, lambda i, vector=vector: vector) for vector in vectors]
        done, arrived = lax.optimization_barrier((work, arrived))
        return arrived

    def placed(first, second, offset):
        own = (place // offset) % 2 == 0
        return jnp.where(own, jnp.stack([first, second]), jnp.stack([second, first]))

    for offset in far:
        held = placed(held, step([crossing(offset, crossed)])[0], offset)
    vectors = [crossing(offset, crossed) for offset in (a, b)]
    over_both, over_a, over_b = step([vectors[0] ^ vectors[1], *vectors])
    held = placed(placed(held, over_b, b), placed(over_a, over_both, b), a)
    (arrived,) = step([1])
    return held, arrived, done


def assemble(held, arrived, weights, cells):
    offsets = halvings(cells)[:-1]
    far, (a, b) = offsets[:-2], offsets[-2:]
    crossed = [*far, b]
    place = lax.axis_index("cell")
    core = place % 2
    for offset in crossed:
        core = core ^ ((place // offset) % 2)
    matrices, rows, _ = held.shape[-3:]
    for k in range(cells // 2):
        at = tuple(2 * k // offset % 2 for offset in (a, b, *reversed(far)))
        first = core == sum(2 * k // offset for offset in crossed) % 2
        for matrix in range(matrices):
            own, other = held[(*at, matrix)], arrived[(*at, matrix)]
            pair = [jnp.where(first, own, other), jnp.where(first, other, own)]
            if rows % 16:
                pair = [part.astype(F32) for part in pair]
            weights[matrix, 2 * k * rows : 2 * (k + 1) * rows, :] = jnp.concatenate(pair, axis=0).astype(BF16)


def reduce_groups(cells):
    left = halvings(cells)[:-1]
    near, middle, farthest = left[-2:], left[1:-2], left[0]
    return near, middle, farthest, [near[0], *middle, farthest]


def reduce_all(keep, send, cells, bricks, across):
    place = lax.axis_index("cell")
    left = halvings(cells)[:-1]
    near, middle, farthest, crossed = reduce_groups(cells)
    total = keep + swap(send, cells, lambda i: 1).astype(F32)
    total = total.reshape((2,) * len(left) + keep.shape[1:])

    def portion(array, flipped):
        for offset, flip in reversed(flipped):
            bit = (place // offset) % 2
            array = lax.dynamic_index_in_dim(array, 1 - bit if flip else bit, left.index(offset), False)
        return array

    def exchange(group):
        nonlocal total, left
        mine = portion(total, [(offset, 0) for offset in group])
        for step in range(1, 1 << len(group)):
            flipped = [(offset, step >> k & 1) for k, offset in enumerate(group)]
            vector = 0
            for offset, flip in flipped:
                vector ^= crossing(offset, crossed) * flip
            sent = portion(total, flipped).astype(BF16)
            mine = mine + swap(sent, cells, lambda i, vector=vector: vector).astype(F32)
        total = mine
        left = [offset for offset in left if offset not in group]

    exchange(near)
    for offset in reversed(middle):
        exchange([offset])

    def meet(array, vector, step):
        pairs = [
            (cell * bricks + brick, (cell ^ vector) * bricks + (brick ^ step))
            for cell in range(cells)
            for brick in range(bricks)
        ]
        return lax.ppermute(array, ("cell", "brick"), pairs).astype(F32)

    vector = crossing(farthest, crossed)
    keep = portion(total, [(farthest, 0)])
    send = portion(total, [(farthest, 1)]).astype(BF16)
    if across:
        keep = keep.astype(BF16)
    total = keep.astype(F32) + meet(send, vector, 0)
    if across:
        far = meet(send, vector, across[0])
        total = total + (far + meet(keep, 0, across[0]))
    for step in across[1:]:
        keep = total.astype(BF16)
        total = keep.astype(F32) + meet(keep, 0, step)
    return total


def body(
    cells,
    bricks,
    features,
    species,
    species_table,
    neighbours,
    counts,
    send_lists,
    distances,
    head_decay,
    norm_gain,
    readout,
    targets,
    master,
    moment,
    second,
):
    atoms, width = features.shape[2:]
    slots = neighbours.shape[2]
    ghost_slots = send_lists.shape[3]
    heads = head_decay.shape[0]
    table_rows = atoms + bricks * ghost_slots

    paired = bricks == 2 and table_rows <= 256
    count = 2 if paired else 1
    brick = lax.axis_index("brick")
    part = table_rows // 2
    own = (features[0, 0], species[0], send_lists[0, 0])
    slot_arrays = (neighbours[0, 0], counts[0], distances[0, 0], targets[0])
    common = (species_table, norm_gain[None])
    embed_shapes = (
        pinned((atoms, width), F32),
        pinned((atoms, width), BF16),
        pinned((width, atoms), BF16),
        pinned((bricks, ghost_slots, width), BF16),
    )
    slot_shapes = tuple(pinned(array.shape, array.dtype) for array in slot_arrays)
    small = pltpu.CompilerParams(vmem_limit_bytes=8 * 1024 * 1024)

    def embed_own():
        rest = (head_decay[None], readout[None], *common)
        shapes = (pinned(master.shape, BF16),) + embed_shapes + slot_shapes
        shapes += tuple(pinned(array.shape, array.dtype) for array in rest)
        if paired:
            shapes += (pinned((width + 4 * slots + PACK_ROWS, atoms), BF16),)
        outs = pl.pallas_call(
            functools.partial(embed_kernel, int(paired)),
            out_shape=shapes,
            in_specs=vmem(6 + len(slot_arrays) + len(rest)),
            out_specs=tuple(vmem(len(shapes))),
            name="embed",
        )(master, *own, *common, *slot_arrays, *rest)
        return outs[0], outs[1:5], outs[5:9], outs[9:13], outs[13:]

    def embed_partner(packed, *common):
        outs = pl.pallas_call(
            unpack_kernel,
            out_shape=embed_shapes + slot_shapes,
            in_specs=vmem(3),
            out_specs=tuple(vmem(8)),
            compiler_params=small,
            name="unpack",
        )(packed, *common)
        return outs[:4], outs[4:]

    def index(first, arrays, decay):
        return pl.pallas_call(
            functools.partial(index_kernel, first),
            out_shape=(pinned((heads, part, atoms), F32), pinned((part, atoms), F32)),
            in_specs=vmem(4),
            out_specs=tuple(vmem(2)),
            scratch_shapes=[pltpu.VMEM((slots, atoms), jnp.int32)],
            compiler_params=small,
            name="index",
        )(*arrays[:3], decay)

    def over_bricks(array, offset):
        return lax.ppermute(array, "brick", [(i, i ^ offset) for i in range(bricks)])

    def ghosts_from(parcel):
        ghosts = parcel
        for offset in range(1, bricks):
            peer = brick ^ offset
            arrived = over_bricks(lax.dynamic_index_in_dim(parcel, peer, 0, True), offset)
            ghosts = lax.dynamic_update_slice_in_dim(ghosts, arrived, peer, 0)
        return ghosts.reshape(bricks * ghost_slots, width)

    def ghosts_of(parcels, place):
        chosen = [lax.dynamic_index_in_dim(parcel, place, 0, False) for parcel in parcels]
        ordered = jnp.where(brick == 0, jnp.stack(chosen), jnp.stack(chosen[::-1]))
        return ordered.reshape(bricks * ghost_slots, width)

    late = []

    shard, state, arrays, (decay, gain, *kept), packed = embed_own()

    def prepare():
        if paired:
            late.extend([over_bricks(packed[0], 1), *kept])
        return state, arrays, decay, gain, index(0, arrays, decay)

    def gather_ghosts(state, arrays, decay, gain, half):
        rows = ghosts_from(state[3])
        return [(state, rows, arrays[3], half, index(part, arrays, decay))], gain

    def visit_partner(state, arrays, decay, gain, half):
        rest = index(part, arrays, decay)
        partner, partner_arrays = embed_partner(*late)
        partner_half = index(0, partner_arrays, decay)
        return (state, arrays[3], half, rest), (partner, partner_arrays, partner_half), decay, gain

    def finish_partner(mine, other, decay, gain):
        state, wanted, half, rest = mine
        partner, arrays, partner_half = other
        parcels = (state[3], partner[3])
        return [
            (state, ghosts_of(parcels, brick), wanted, half, rest),
            (partner, ghosts_of(parcels, 1 - brick), arrays[3], partner_half, index(part, arrays, decay)),
        ], gain

    steps = [prepare, *[lambda *done: done] * (len(halvings(cells)) - 4)]
    steps += [visit_partner, finish_partner] if paired else [gather_ghosts]
    held, arrived, (worked, gain) = gather_cells(shard, cells, steps)
    operands = []
    for (embedded, normed, normed_t, _), ghosts, wanted, half, rest in worked:
        operands += [normed, normed_t, ghosts, embedded, *half, *rest, wanted]

    columns = heads * atoms
    blocks = (cells // 2,) + master.shape
    energies, keep, send = pl.pallas_call(
        functools.partial(sweep_kernel, count, cells),
        out_shape=(struct((1, atoms), F32), pinned(blocks, F32), pinned(blocks, BF16)),
        in_specs=vmem(3 + len(operands)),
        out_specs=tuple(vmem(3)),
        scratch_shapes=[
            pltpu.VMEM((table_rows, columns), F32),
            pltpu.VMEM((table_rows, columns), F32),
            pltpu.VMEM((table_rows, columns), BF16),
            pltpu.VMEM((table_rows, columns), BF16),
        ]
        * count
        + [pltpu.VMEM((master.shape[0], width, width), BF16)],
        compiler_params=pltpu.CompilerParams(vmem_limit_bytes=32 * 1024 * 1024),
        name="sweep",
    )(held, arrived, gain, *operands)

    across = [] if paired else list(reversed(halvings(bricks)))
    owned = reduce_all(keep, send, cells, bricks, across)
    moment_new = 0.9 * moment + 0.1 * owned
    second_new = 0.999 * second + 0.001 * owned * owned
    adam_step = moment_new / (jnp.sqrt(second_new) + 1e-08)
    return (energies[None], moment_new, second_new, adam_step)


def solution(mesh):
    return jax.shard_map(
        functools.partial(body, mesh.shape["cell"], mesh.shape["brick"]),
        mesh=mesh,
        in_specs=(
            P("cell", "brick", None, None),
            P("cell", "brick", None),
            P(),
            P("cell", "brick", None, None),
            P("cell", "brick", None),
            P("cell", "brick", None, None),
            P("cell", "brick", None, None),
            P(),
            P(),
            P(),
            P("cell", "brick", None),
            P(None, "cell", None),
            P(None, "cell", None),
            P(None, "cell", None),
        ),
        out_specs=(
            P("cell", "brick", None),
            P(None, "cell", None),
            P(None, "cell", None),
            P(None, "cell", None),
        ),
        check_vma=False,
    )
```

```python
import functools
import math

import jax
import jax.numpy as jnp
from jax import lax
from jax.experimental import pallas as pl
from jax.experimental.pallas import tpu as pltpu
from jax.sharding import PartitionSpec as P

CHUNK = 32
DEPTH = 5
FAR = 1e30
FAR_ROW = 1 << 20
PACK_ROWS = 16

loss_weight = 0.0625
epsilon_norm = 1e-06

F32 = jnp.float32
BF16 = jnp.bfloat16
NT = (((1,), (1,)), ((), ()))
TN = (((0,), (0,)), ((), ()))


def dot(a, b):
    return jnp.dot(a, b, preferred_element_type=F32)


def dot_nt(a, b):
    return lax.dot_general(a, b, NT, preferred_element_type=F32)


def dot_tn(a, b):
    return lax.dot_general(a, b, TN, preferred_element_type=F32)


def to_column(row):
    n = row.shape[1]
    eye = lax.broadcasted_iota(jnp.int32, (n, n), 0) == lax.broadcasted_iota(jnp.int32, (n, n), 1)
    return jnp.sum(jnp.where(eye, row, jnp.zeros_like(row)), axis=1, keepdims=True)


def to_row(column):
    n = column.shape[0]
    eye = lax.broadcasted_iota(jnp.int32, (n, n), 0) == lax.broadcasted_iota(jnp.int32, (n, n), 1)
    return jnp.sum(jnp.where(eye, column, jnp.zeros_like(column)), axis=0, keepdims=True)


def embed(features, species, species_table, norm_gain, send_rows, embedded, normed, normed_t, parcel):
    atoms = features.shape[0]
    column = to_column(species)
    picked = jnp.zeros_like(features)
    for kind in range(species_table.shape[0]):
        row = species_table[kind : kind + 1, :].astype(F32)
        picked = jnp.where(column == kind, row, picked)
    total = features + picked
    embedded[...] = total
    scale = lax.rsqrt(jnp.mean(total * total, axis=-1, keepdims=True) + epsilon_norm)
    norm = total * scale * norm_gain[...]
    half = norm.astype(BF16)
    normed[...] = half
    normed_t[...] = norm.T.astype(BF16)
    bricks, slots = send_rows.shape
    for brick in range(bricks):
        chosen = send_rows[brick : brick + 1, :]
        picks = (lax.broadcasted_iota(jnp.int32, (atoms, slots), 0) == chosen).astype(F32).astype(BF16)
        parcel[brick] = dot_tn(picks, half).astype(BF16)


def terms_of(value):
    high = value.astype(BF16).astype(F32)
    rest = value - high
    middle = rest.astype(BF16).astype(F32)
    return [high, middle, rest - middle]


def embed_kernel(pack, master, features, species, send_rows, species_table, norm_gain, *refs):
    count = (len(refs) - 5 - pack) // 2
    sources, (shard, embedded, normed, normed_t, parcel) = refs[:count], refs[count : count + 5]
    kept = refs[count + 5 :]
    shard[...] = master[...].astype(BF16)
    for source, target in zip(sources, kept):
        target[...] = source[...]
    if pack:
        neighbours, counts, distances, targets = sources[:4]
        packed = kept[-1]
        slots, atoms = neighbours.shape
        width = features.shape[1]
        arrays = [features[:, at : at + atoms].astype(F32) for at in range(0, width, atoms)]
        arrays += [neighbours[...].astype(F32), *terms_of(distances[...])]
        bricks, sent = send_rows.shape
        rows = [species[...].astype(F32), counts[...].astype(F32), *terms_of(targets[...])]
        lists = jnp.concatenate([send_rows[...].astype(F32), jnp.zeros((bricks, atoms - sent), F32)], axis=1)
        rows += [lists, jnp.zeros((PACK_ROWS - len(rows) - bricks, atoms), F32)]
        start = 0
        for array in [*arrays, jnp.concatenate(rows, axis=0)]:
            packed[start : start + array.shape[0], :] = array.astype(BF16)
            start += array.shape[0]
    embed(features[...].astype(F32), species[...], species_table, norm_gain, send_rows, embedded, normed, normed_t, parcel)


def unpack_kernel(packed, species_table, norm_gain, embedded, normed, normed_t, parcel, neighbours, counts, distances, targets):
    slots, atoms = neighbours.shape
    width = embedded.shape[1]
    bricks, sent = parcel.shape[:2]
    start = 0

    def take(rows):
        nonlocal start
        start += rows
        return packed[start - rows : start, :].astype(F32)

    features = jnp.concatenate([take(atoms) for _ in range(width // atoms)], axis=1)
    neighbours[...] = take(slots).astype(jnp.int32)
    distances[...] = take(slots) + take(slots) + take(slots)
    rows = take(PACK_ROWS)
    counts[...] = rows[1:2].astype(jnp.int32)
    targets[...] = rows[2:3] + rows[3:4] + rows[4:5]
    send_rows = rows[5 : 5 + bricks, :sent].astype(jnp.int32)
    species = rows[0:1].astype(jnp.int32)
    embed(features, species, species_table, norm_gain, send_rows, embedded, normed, normed_t, parcel)


def index_kernel(first, neighbours, counts, distances, decay, weight, absent, key_ref):
    slots, atoms = neighbours.shape
    heads, table_rows = weight.shape[:2]
    slot = lax.broadcasted_iota(jnp.int32, (slots, atoms), 0)
    valid = slot < counts[...]
    held = jnp.where(valid, neighbours[...] - first, -FAR_ROW - slot)
    key_ref[...] = held
    slope = [-decay[:, h : h + 1] for h in range(heads)]

    def chunk(step, nearest):
        start = pl.multiple_of(step * CHUNK, CHUNK)
        at = pl.ds(start, CHUNK)
        row = lax.broadcasted_iota(jnp.int32, (CHUNK, atoms), 0) + start
        layers = [jnp.full((CHUNK, atoms), FAR, F32) for _ in range(DEPTH)]
        for j in range(slots):
            hit = row == key_ref[j : j + 1, :]
            entering = distances[j : j + 1, :]
            for k in range(DEPTH):
                entering, layers[k] = layers[k], jnp.where(hit, entering, layers[k])
        absent[at, :] = jnp.where(layers[0] < FAR, 0.0, -FAR)
        for h in range(heads):
            weight[h, at, :] = sum(jnp.exp(slope[h] * layer) for layer in layers)
        return jnp.minimum(nearest, jnp.min(layers[-1], axis=0, keepdims=True))

    nearest = lax.fori_loop(0, table_rows // CHUNK, chunk, jnp.full((1, atoms), FAR, F32))

    @pl.when(jnp.min(nearest) < FAR)
    def _():
        rank = jnp.zeros((slots, atoms), jnp.int32)
        for j in range(slots):
            rank += ((held == key_ref[j : j + 1, :]) & (slot < j)).astype(jnp.int32)
        inside = valid & (held >= 0) & (held < table_rows)
        key_ref[...] = jnp.where(inside, held + table_rows * rank, -1)

        def layer(level, carry):
            for start in range(0, table_rows, CHUNK):
                at = pl.ds(start, CHUNK)
                row = lax.broadcasted_iota(jnp.int32, (CHUNK, atoms), 0) + (start + level * table_rows)
                distance = jnp.full((CHUNK, atoms), FAR, F32)
                for j in range(slots):
                    distance = jnp.where(row == key_ref[j : j + 1, :], distances[j : j + 1, :], distance)
                for h in range(heads):
                    weight[h, at, :] += jnp.exp(slope[h] * distance)
            return carry

        lax.fori_loop(DEPTH, jnp.max(rank) + 1, layer, 0)


def sweep_kernel(count, cells, held, arrived, readout, *refs):
    operands, scratch = 9, 4
    energies, keep, send = refs[operands * count : operands * count + 3]
    bricks = [refs[operands * i : operands * (i + 1)] for i in range(count)]
    start = operands * count + 3
    weights = refs[-1]
    assemble(held, arrived, weights, cells)
    memory = [refs[start + scratch * i : start + scratch * (i + 1)] for i in range(count)]
    atoms, width = bricks[0][0].shape
    heads = bricks[0][4].shape[0]
    head_size = width // heads
    scale = 1.0 / math.sqrt(head_size)
    head_of = lax.broadcasted_iota(jnp.int32, (atoms, width), 1) // head_size
    group = math.gcd(heads, 2)
    out_proj = weights[3]

    def stacked(array):
        zero = jnp.zeros_like(array)
        return jnp.concatenate([jnp.where(head_of == h, array, zero) for h in range(heads)], axis=0)

    def own_channels(turned, blocks, h):
        channels = turned[h * head_size : (h + group) * head_size]
        wide = dot(channels, blocks[:, h * atoms : (h + group) * atoms])
        return [wide[i * head_size : (i + 1) * head_size, i * atoms : (i + 1) * atoms] for i in range(group)]

    def work(i):
        normed, normed_t, ghosts, embedded, weight, absent, weight_rest, absent_rest, targets = bricks[i]
        score_ref, att_ref, att_half, grad_score = memory[i]
        norm = normed[...]
        table = jnp.concatenate([norm, ghosts[...]], axis=0)
        query = stacked(dot(norm, weights[0]).astype(BF16))
        keys = dot(table, weights[1])
        values = dot(table, weights[2])
        yield
        keys_t, values_t = keys.T.astype(BF16), values.T.astype(BF16)
        keys, values = keys.astype(BF16), values.astype(BF16)
        score_ref[...] = dot_nt(keys, query)
        yield
        gone = jnp.concatenate([absent[...], absent_rest[...]], axis=0)
        parts = []
        for h in range(heads):
            at = pl.ds(h * atoms, atoms)
            score = score_ref[:, at] + gone
            weights_h = jnp.concatenate([weight[h], weight_rest[h]], axis=0)
            score = (score - jnp.max(score, axis=0, keepdims=True)) * (scale * math.log2(math.e))
            terms = jnp.exp2(score) * weights_h
            attention = terms * (1.0 / jnp.sum(terms, axis=0, keepdims=True))
            att_ref[:, at] = attention
            att_half[:, at] = attention.astype(BF16)
            if h % group == group - 1:
                parts += own_channels(values_t, att_half, h - group + 1)
        attended_t = jnp.concatenate(parts, axis=0)
        yield
        updated = embedded[...] + dot(attended_t.T.astype(BF16), out_proj)
        sigmoid = 1.0 / (1.0 + jnp.exp(-updated))
        energy = jnp.sum(readout[...] * (updated * sigmoid), axis=1, keepdims=True)
        if i == 0:
            energies[...] = to_row(energy)
        grad_energy = loss_weight * (energy - to_column(targets[...]))
        slope = sigmoid * (1.0 + updated * (1.0 - sigmoid))
        grad_updated = (grad_energy * readout[...] * slope).astype(BF16)
        yield
        grad_out = dot(attended_t.astype(BF16), grad_updated)
        grad_attended = stacked(dot_nt(grad_updated, out_proj).astype(BF16))
        yield
        score_ref[...] = dot_nt(values, grad_attended)
        yield
        table_t = jnp.concatenate([normed_t[...], ghosts[...].astype(F32).T.astype(BF16)], axis=1)
        value_grads = dot(att_half[...], grad_attended)
        grad_value = dot(table_t, value_grads.astype(BF16))
        yield
        parts = []
        for h in range(heads):
            at = pl.ds(h * atoms, atoms)
            attention = att_ref[:, at]
            grad_weights = score_ref[:, at]
            mean = jnp.sum(attention * grad_weights, axis=0, keepdims=True)
            grad_score[:, at] = (attention * (grad_weights - mean)).astype(BF16)
            if h % group == group - 1:
                parts += own_channels(keys_t, grad_score, h - group + 1)
        yield
        key_grads = dot(grad_score[...], query) * scale
        yield
        grad_query_t = jnp.concatenate(parts, axis=0) * scale
        grad_query = dot_nt(normed_t[...], grad_query_t.astype(BF16))
        yield grad_query, dot(table_t, key_grads.astype(BF16)), grad_value, grad_out

    running = [work(i) for i in range(count)]
    found = [None] * count
    while found[0] is None:
        found = [next(step) for step in running]
    crossed = reduce_groups(cells)[3]
    place = lax.axis_index("cell")
    core = place % 2
    for offset in crossed:
        core = core ^ ((place // offset) % 2)
    for matrix in range(4):
        total = sum(part[matrix] for part in found[1:]) + found[0][matrix]
        blocks = total.reshape((cells // 2, 2) + keep.shape[2:])
        for k in range(cells // 2):
            first = core == sum(2 * k // offset for offset in crossed) % 2
            keep[k, matrix] = jnp.where(first, blocks[k, 0], blocks[k, 1])
            send[k, matrix] = jnp.where(first, blocks[k, 1], blocks[k, 0]).astype(BF16)


def vmem(count):
    return [pl.BlockSpec(memory_space=pltpu.VMEM)] * count


SMEM = pl.BlockSpec(memory_space=pltpu.SMEM)


def struct(shape, dtype):
    return jax.ShapeDtypeStruct(shape, dtype)


def pinned(shape, dtype):
    return pltpu.VMEM(shape, dtype)


def halvings(size):
    offsets = []
    offset = size // 2
    while offset:
        offsets.append(offset)
        offset //= 2
    return offsets


def crossing(offset, crossed):
    return offset | 1 if offset in crossed else offset


def swap(array, cells, vector_of):
    return lax.ppermute(array, "cell", [(i, i ^ vector_of(i)) for i in range(cells)])


def gather_cells(shard, cells, beside):
    place = lax.axis_index("cell")
    offsets = halvings(cells)[:-1]
    far, (a, b) = offsets[:-2], offsets[-2:]
    crossed = [*far, b]
    held = shard
    done = ()

    def step(vectors):
        nonlocal done
        work = beside.pop(0)(*done) if beside else done
        arrived = [swap(held, cells, lambda i, vector=vector: vector) for vector in vectors]
        done, arrived = lax.optimization_barrier((work, arrived))
        return arrived

    def placed(first, second, offset):
        own = (place // offset) % 2 == 0
        return jnp.where(own, jnp.stack([first, second]), jnp.stack([second, first]))

    for offset in far:
        held = placed(held, step([crossing(offset, crossed)])[0], offset)
    vectors = [crossing(offset, crossed) for offset in (a, b)]
    over_both, over_a, over_b = step([vectors[0] ^ vectors[1], *vectors])
    held = placed(placed(held, over_b, b), placed(over_a, over_both, b), a)
    (arrived,) = step([1])
    return held, arrived, done


def assemble(held, arrived, weights, cells):
    offsets = halvings(cells)[:-1]
    far, (a, b) = offsets[:-2], offsets[-2:]
    crossed = [*far, b]
    place = lax.axis_index("cell")
    core = place % 2
    for offset in crossed:
        core = core ^ ((place // offset) % 2)
    matrices, rows, _ = held.shape[-3:]
    for k in range(cells // 2):
        at = tuple(2 * k // offset % 2 for offset in (a, b, *reversed(far)))
        first = core == sum(2 * k // offset for offset in crossed) % 2
        for matrix in range(matrices):
            own, other = held[(*at, matrix)], arrived[(*at, matrix)]
            pair = [jnp.where(first, own, other), jnp.where(first, other, own)]
            if rows % 16:
                pair = [part.astype(F32) for part in pair]
            weights[matrix, 2 * k * rows : 2 * (k + 1) * rows, :] = jnp.concatenate(pair, axis=0).astype(BF16)


def reduce_groups(cells):
    left = halvings(cells)[:-1]
    near, middle, farthest = left[-2:], left[1:-2], left[0]
    return near, middle, farthest, [near[0], *middle, farthest]


def reduce_all(keep, send, cells, bricks, across):
    place = lax.axis_index("cell")
    left = halvings(cells)[:-1]
    near, middle, farthest, crossed = reduce_groups(cells)
    total = keep + swap(send, cells, lambda i: 1).astype(F32)
    total = total.reshape((2,) * len(left) + keep.shape[1:])

    def portion(array, flipped):
        for offset, flip in reversed(flipped):
            bit = (place // offset) % 2
            array = lax.dynamic_index_in_dim(array, 1 - bit if flip else bit, left.index(offset), False)
        return array

    def exchange(group):
        nonlocal total, left
        mine = portion(total, [(offset, 0) for offset in group])
        for step in (2, 3, 1) if len(group) == 2 else (1,):
            flipped = [(offset, step >> k & 1) for k, offset in enumerate(group)]
            vector = 0
            for offset, flip in flipped:
                vector ^= crossing(offset, crossed) * flip
            sent = portion(total, flipped).astype(BF16)
            mine = mine + swap(sent, cells, lambda i, vector=vector: vector).astype(F32)
        total = mine
        left = [offset for offset in left if offset not in group]

    exchange(near)
    for offset in reversed(middle):
        exchange([offset])

    def meet(array, vector, step):
        pairs = [
            (cell * bricks + brick, (cell ^ vector) * bricks + (brick ^ step))
            for cell in range(cells)
            for brick in range(bricks)
        ]
        return lax.ppermute(array, ("cell", "brick"), pairs).astype(F32)

    vector = crossing(farthest, crossed)
    keep = portion(total, [(farthest, 0)])
    send = portion(total, [(farthest, 1)]).astype(BF16)
    if across:
        keep = keep.astype(BF16)
    total = keep.astype(F32) + meet(send, vector, 0)
    if across:
        far = meet(send, vector, across[0])
        total = total + (far + meet(keep, 0, across[0]))
    for step in across[1:]:
        keep = total.astype(BF16)
        total = keep.astype(F32) + meet(keep, 0, step)
    return total


def body(
    cells,
    bricks,
    features,
    species,
    species_table,
    neighbours,
    counts,
    send_lists,
    distances,
    head_decay,
    norm_gain,
    readout,
    targets,
    master,
    moment,
    second,
):
    atoms, width = features.shape[2:]
    slots = neighbours.shape[2]
    ghost_slots = send_lists.shape[3]
    heads = head_decay.shape[0]
    table_rows = atoms + bricks * ghost_slots

    paired = bricks == 2 and table_rows <= 256
    count = 2 if paired else 1
    brick = lax.axis_index("brick")
    part = table_rows // 2
    own = (features[0, 0], species[0], send_lists[0, 0])
    slot_arrays = (neighbours[0, 0], counts[0], distances[0, 0], targets[0])
    common = (species_table, norm_gain[None])
    embed_shapes = (
        pinned((atoms, width), F32),
        pinned((atoms, width), BF16),
        pinned((width, atoms), BF16),
        pinned((bricks, ghost_slots, width), BF16),
    )
    slot_shapes = tuple(pinned(array.shape, array.dtype) for array in slot_arrays)
    small = pltpu.CompilerParams(vmem_limit_bytes=8 * 1024 * 1024)

    def embed_own():
        rest = (head_decay[None], readout[None], *common)
        shapes = (pinned(master.shape, BF16),) + embed_shapes + slot_shapes
        shapes += tuple(pinned(array.shape, array.dtype) for array in rest)
        if paired:
            shapes += (pinned((width + 4 * slots + PACK_ROWS, atoms), BF16),)
        outs = pl.pallas_call(
            functools.partial(embed_kernel, int(paired)),
            out_shape=shapes,
            in_specs=vmem(6 + len(slot_arrays) + len(rest)),
            out_specs=tuple(vmem(len(shapes))),
            name="embed",
        )(master, *own, *common, *slot_arrays, *rest)
        return outs[0], outs[1:5], outs[5:9], outs[9:13], outs[13:]

    def embed_partner(packed, *common):
        outs = pl.pallas_call(
            unpack_kernel,
            out_shape=embed_shapes + slot_shapes,
            in_specs=vmem(3),
            out_specs=tuple(vmem(8)),
            compiler_params=small,
            name="unpack",
        )(packed, *common)
        return outs[:4], outs[4:]

    def index(first, arrays, decay):
        return pl.pallas_call(
            functools.partial(index_kernel, first),
            out_shape=(pinned((heads, part, atoms), F32), pinned((part, atoms), F32)),
            in_specs=vmem(4),
            out_specs=tuple(vmem(2)),
            scratch_shapes=[pltpu.VMEM((slots, atoms), jnp.int32)],
            compiler_params=small,
            name="index",
        )(*arrays[:3], decay)

    def over_bricks(array, offset):
        return lax.ppermute(array, "brick", [(i, i ^ offset) for i in range(bricks)])

    def ghosts_from(parcel):
        ghosts = parcel
        for offset in range(1, bricks):
            peer = brick ^ offset
            arrived = over_bricks(lax.dynamic_index_in_dim(parcel, peer, 0, True), offset)
            ghosts = lax.dynamic_update_slice_in_dim(ghosts, arrived, peer, 0)
        return ghosts.reshape(bricks * ghost_slots, width)

    def ghosts_of(parcels, place):
        chosen = [lax.dynamic_index_in_dim(parcel, place, 0, False) for parcel in parcels]
        ordered = jnp.where(brick == 0, jnp.stack(chosen), jnp.stack(chosen[::-1]))
        return ordered.reshape(bricks * ghost_slots, width)

    late = []

    shard, state, arrays, (decay, gain, *kept), packed = embed_own()

    def prepare():
        if paired:
            late.extend([over_bricks(packed[0], 1), *kept])
        return state, arrays, decay, gain, index(0, arrays, decay)

    def gather_ghosts(state, arrays, decay, gain, half):
        rows = ghosts_from(state[3])
        return [(state, rows, arrays[3], half, index(part, arrays, decay))], gain

    def visit_partner(state, arrays, decay, gain, half):
        rest = index(part, arrays, decay)
        partner, partner_arrays = embed_partner(*late)
        partner_half = index(0, partner_arrays, decay)
        return (state, arrays[3], half, rest), (partner, partner_arrays, partner_half), decay, gain

    def finish_partner(mine, other, decay, gain):
        state, wanted, half, rest = mine
        partner, arrays, partner_half = other
        parcels = (state[3], partner[3])
        return [
            (state, ghosts_of(parcels, brick), wanted, half, rest),
            (partner, ghosts_of(parcels, 1 - brick), arrays[3], partner_half, index(part, arrays, decay)),
        ], gain

    steps = [prepare, *[lambda *done: done] * (len(halvings(cells)) - 4)]
    steps += [visit_partner, finish_partner] if paired else [gather_ghosts]
    held, arrived, (worked, gain) = gather_cells(shard, cells, steps)
    operands = []
    for (embedded, normed, normed_t, _), ghosts, wanted, half, rest in worked:
        operands += [normed, normed_t, ghosts, embedded, *half, *rest, wanted]

    columns = heads * atoms
    blocks = (cells // 2,) + master.shape
    energies, keep, send = pl.pallas_call(
        functools.partial(sweep_kernel, count, cells),
        out_shape=(struct((1, atoms), F32), pinned(blocks, F32), pinned(blocks, BF16)),
        in_specs=vmem(3 + len(operands)),
        out_specs=tuple(vmem(3)),
        scratch_shapes=[
            pltpu.VMEM((table_rows, columns), F32),
            pltpu.VMEM((table_rows, columns), F32),
            pltpu.VMEM((table_rows, columns), BF16),
            pltpu.VMEM((table_rows, columns), BF16),
        ]
        * count
        + [pltpu.VMEM((master.shape[0], width, width), BF16)],
        compiler_params=pltpu.CompilerParams(vmem_limit_bytes=32 * 1024 * 1024),
        name="sweep",
    )(held, arrived, gain, *operands)

    across = [] if paired else list(reversed(halvings(bricks)))
    owned = reduce_all(keep, send, cells, bricks, across)
    moment_new = 0.9 * moment + 0.1 * owned
    second_new = 0.999 * second + 0.001 * owned * owned
    adam_step = moment_new / (jnp.sqrt(second_new) + 1e-08)
    return (energies[None], moment_new, second_new, adam_step)


def solution(mesh):
    return jax.shard_map(
        functools.partial(body, mesh.shape["cell"], mesh.shape["brick"]),
        mesh=mesh,
        in_specs=(
            P("cell", "brick", None, None),
            P("cell", "brick", None),
            P(),
            P("cell", "brick", None, None),
            P("cell", "brick", None),
            P("cell", "brick", None, None),
            P("cell", "brick", None, None),
            P(),
            P(),
            P(),
            P("cell", "brick", None),
            P(None, "cell", None),
            P(None, "cell", None),
            P(None, "cell", None),
        ),
        out_specs=(
            P("cell", "brick", None),
            P(None, "cell", None),
            P(None, "cell", None),
            P(None, "cell", None),
        ),
        check_vma=False,
    )
```

```python
import functools
import math

import jax
import jax.numpy as jnp
from jax import lax
from jax.experimental import pallas as pl
from jax.experimental.pallas import tpu as pltpu
from jax.sharding import PartitionSpec as P

CHUNK = 32
DEPTH = 5
FAR = 1e30
FAR_ROW = 1 << 20
PACK_ROWS = 16

loss_weight = 0.0625
epsilon_norm = 1e-06

F32 = jnp.float32
BF16 = jnp.bfloat16
NT = (((1,), (1,)), ((), ()))
TN = (((0,), (0,)), ((), ()))


def dot(a, b):
    return jnp.dot(a, b, preferred_element_type=F32)


def dot_nt(a, b):
    return lax.dot_general(a, b, NT, preferred_element_type=F32)


def dot_tn(a, b):
    return lax.dot_general(a, b, TN, preferred_element_type=F32)


def to_column(row):
    n = row.shape[1]
    eye = lax.broadcasted_iota(jnp.int32, (n, n), 0) == lax.broadcasted_iota(jnp.int32, (n, n), 1)
    return jnp.sum(jnp.where(eye, row, jnp.zeros_like(row)), axis=1, keepdims=True)


def to_row(column):
    n = column.shape[0]
    eye = lax.broadcasted_iota(jnp.int32, (n, n), 0) == lax.broadcasted_iota(jnp.int32, (n, n), 1)
    return jnp.sum(jnp.where(eye, column, jnp.zeros_like(column)), axis=0, keepdims=True)


def embed(features, species, species_table, norm_gain, send_rows, embedded, normed, normed_t, parcel):
    atoms = features.shape[0]
    column = to_column(species)
    picked = jnp.zeros_like(features)
    for kind in range(species_table.shape[0]):
        row = species_table[kind : kind + 1, :].astype(F32)
        picked = jnp.where(column == kind, row, picked)
    total = features + picked
    embedded[...] = total
    scale = lax.rsqrt(jnp.mean(total * total, axis=-1, keepdims=True) + epsilon_norm)
    norm = total * scale * norm_gain[...]
    half = norm.astype(BF16)
    normed[...] = half
    normed_t[...] = norm.T.astype(BF16)
    bricks, slots = send_rows.shape
    for brick in range(bricks):
        chosen = send_rows[brick : brick + 1, :]
        picks = (lax.broadcasted_iota(jnp.int32, (atoms, slots), 0) == chosen).astype(F32).astype(BF16)
        parcel[brick] = dot_tn(picks, half).astype(BF16)


def terms_of(value):
    high = value.astype(BF16).astype(F32)
    rest = value - high
    middle = rest.astype(BF16).astype(F32)
    return [high, middle, rest - middle]


def embed_kernel(pack, master, features, species, send_rows, species_table, norm_gain, *refs):
    count = (len(refs) - 5 - pack) // 2
    sources, (shard, embedded, normed, normed_t, parcel) = refs[:count], refs[count : count + 5]
    kept = refs[count + 5 :]
    shard[...] = master[...].astype(BF16)
    for source, target in zip(sources, kept):
        target[...] = source[...]
    if pack:
        neighbours, counts, distances, targets = sources[:4]
        packed = kept[-1]
        slots, atoms = neighbours.shape
        width = features.shape[1]
        arrays = [features[:, at : at + atoms].astype(F32) for at in range(0, width, atoms)]
        arrays += [neighbours[...].astype(F32), *terms_of(distances[...])]
        bricks, sent = send_rows.shape
        rows = [species[...].astype(F32), counts[...].astype(F32), *terms_of(targets[...])]
        lists = jnp.concatenate([send_rows[...].astype(F32), jnp.zeros((bricks, atoms - sent), F32)], axis=1)
        rows += [lists, jnp.zeros((PACK_ROWS - len(rows) - bricks, atoms), F32)]
        start = 0
        for array in [*arrays, jnp.concatenate(rows, axis=0)]:
            packed[start : start + array.shape[0], :] = array.astype(BF16)
            start += array.shape[0]
    embed(features[...].astype(F32), species[...], species_table, norm_gain, send_rows, embedded, normed, normed_t, parcel)


def unpack_kernel(packed, species_table, norm_gain, embedded, normed, normed_t, parcel, neighbours, counts, distances, targets):
    slots, atoms = neighbours.shape
    width = embedded.shape[1]
    bricks, sent = parcel.shape[:2]
    start = 0

    def take(rows):
        nonlocal start
        start += rows
        return packed[start - rows : start, :].astype(F32)

    features = jnp.concatenate([take(atoms) for _ in range(width // atoms)], axis=1)
    neighbours[...] = take(slots).astype(jnp.int32)
    distances[...] = take(slots) + take(slots) + take(slots)
    rows = take(PACK_ROWS)
    counts[...] = rows[1:2].astype(jnp.int32)
    targets[...] = rows[2:3] + rows[3:4] + rows[4:5]
    send_rows = rows[5 : 5 + bricks, :sent].astype(jnp.int32)
    species = rows[0:1].astype(jnp.int32)
    embed(features, species, species_table, norm_gain, send_rows, embedded, normed, normed_t, parcel)


def index_kernel(first, neighbours, counts, distances, decay, weight, absent, key_ref):
    slots, atoms = neighbours.shape
    heads, table_rows = weight.shape[:2]
    slot = lax.broadcasted_iota(jnp.int32, (slots, atoms), 0)
    valid = slot < counts[...]
    held = jnp.where(valid, neighbours[...] - first, -FAR_ROW - slot)
    key_ref[...] = held
    slope = [-decay[:, h : h + 1] for h in range(heads)]

    def chunk(step, nearest):
        start = pl.multiple_of(step * CHUNK, CHUNK)
        at = pl.ds(start, CHUNK)
        row = lax.broadcasted_iota(jnp.int32, (CHUNK, atoms), 0) + start
        layers = [jnp.full((CHUNK, atoms), FAR, F32) for _ in range(DEPTH)]
        for j in range(slots):
            hit = row == key_ref[j : j + 1, :]
            entering = distances[j : j + 1, :]
            for k in range(DEPTH):
                entering, layers[k] = layers[k], jnp.where(hit, entering, layers[k])
        absent[at, :] = jnp.where(layers[0] < FAR, 0.0, -FAR)
        for h in range(heads):
            weight[h, at, :] = sum(jnp.exp(slope[h] * layer) for layer in layers)
        return jnp.minimum(nearest, jnp.min(layers[-1], axis=0, keepdims=True))

    nearest = lax.fori_loop(0, table_rows // CHUNK, chunk, jnp.full((1, atoms), FAR, F32))

    @pl.when(jnp.min(nearest) < FAR)
    def _():
        rank = jnp.zeros((slots, atoms), jnp.int32)
        for j in range(slots):
            rank += ((held == key_ref[j : j + 1, :]) & (slot < j)).astype(jnp.int32)
        inside = valid & (held >= 0) & (held < table_rows)
        key_ref[...] = jnp.where(inside, held + table_rows * rank, -1)

        def layer(level, carry):
            for start in range(0, table_rows, CHUNK):
                at = pl.ds(start, CHUNK)
                row = lax.broadcasted_iota(jnp.int32, (CHUNK, atoms), 0) + (start + level * table_rows)
                distance = jnp.full((CHUNK, atoms), FAR, F32)
                for j in range(slots):
                    distance = jnp.where(row == key_ref[j : j + 1, :], distances[j : j + 1, :], distance)
                for h in range(heads):
                    weight[h, at, :] += jnp.exp(slope[h] * distance)
            return carry

        lax.fori_loop(DEPTH, jnp.max(rank) + 1, layer, 0)


def sweep_kernel(count, cells, held, arrived, readout, *refs):
    operands, scratch = 9, 4
    energies, keep, send = refs[operands * count : operands * count + 3]
    bricks = [refs[operands * i : operands * (i + 1)] for i in range(count)]
    start = operands * count + 3
    weights = refs[-1]
    assemble(held, arrived, weights, cells)
    memory = [refs[start + scratch * i : start + scratch * (i + 1)] for i in range(count)]
    atoms, width = bricks[0][0].shape
    heads = bricks[0][4].shape[0]
    head_size = width // heads
    scale = 1.0 / math.sqrt(head_size)
    head_of = lax.broadcasted_iota(jnp.int32, (atoms, width), 1) // head_size
    group = math.gcd(heads, 2)
    out_proj = weights[3]

    def stacked(array):
        zero = jnp.zeros_like(array)
        return jnp.concatenate([jnp.where(head_of == h, array, zero) for h in range(heads)], axis=0)

    def own_channels(turned, blocks, h):
        channels = turned[h * head_size : (h + group) * head_size]
        wide = dot(channels, blocks[:, h * atoms : (h + group) * atoms])
        return [wide[i * head_size : (i + 1) * head_size, i * atoms : (i + 1) * atoms] for i in range(group)]

    def work(i):
        normed, normed_t, ghosts, embedded, weight, absent, weight_rest, absent_rest, targets = bricks[i]
        score_ref, att_ref, att_half, grad_score = memory[i]
        norm = normed[...]
        table = jnp.concatenate([norm, ghosts[...]], axis=0)
        query = stacked(dot(norm, weights[0]).astype(BF16))
        keys = dot(table, weights[1])
        values = dot(table, weights[2])
        yield
        keys_t, values_t = keys.T.astype(BF16), values.T.astype(BF16)
        keys, values = keys.astype(BF16), values.astype(BF16)
        score_ref[...] = dot_nt(keys, query)
        yield
        gone = jnp.concatenate([absent[...], absent_rest[...]], axis=0)
        parts = []
        for h in range(heads):
            at = pl.ds(h * atoms, atoms)
            score = score_ref[:, at] + gone
            weights_h = jnp.concatenate([weight[h], weight_rest[h]], axis=0)
            score = (score - jnp.max(score, axis=0, keepdims=True)) * (scale * math.log2(math.e))
            terms = jnp.exp2(score) * weights_h
            attention = terms * (1.0 / jnp.sum(terms, axis=0, keepdims=True))
            att_ref[:, at] = attention
            att_half[:, at] = attention.astype(BF16)
            if h % group == group - 1:
                parts += own_channels(values_t, att_half, h - group + 1)
        attended_t = jnp.concatenate(parts, axis=0)
        yield
        updated = embedded[...] + dot(attended_t.T.astype(BF16), out_proj)
        sigmoid = 1.0 / (1.0 + jnp.exp(-updated))
        energy = jnp.sum(readout[...] * (updated * sigmoid), axis=1, keepdims=True)
        if i == 0:
            energies[...] = to_row(energy)
        grad_energy = loss_weight * (energy - to_column(targets[...]))
        slope = sigmoid * (1.0 + updated * (1.0 - sigmoid))
        grad_updated = (grad_energy * readout[...] * slope).astype(BF16)
        yield
        grad_out = dot(attended_t.astype(BF16), grad_updated)
        grad_attended = stacked(dot_nt(grad_updated, out_proj).astype(BF16))
        yield
        score_ref[...] = dot_nt(values, grad_attended)
        yield
        table_t = jnp.concatenate([normed_t[...], ghosts[...].astype(F32).T.astype(BF16)], axis=1)
        value_grads = dot(att_half[...], grad_attended)
        grad_value = dot(table_t, value_grads.astype(BF16))
        yield
        parts = []
        for h in range(heads):
            at = pl.ds(h * atoms, atoms)
            attention = att_ref[:, at]
            grad_weights = score_ref[:, at]
            mean = jnp.sum(attention * grad_weights, axis=0, keepdims=True)
            grad_score[:, at] = (attention * (grad_weights - mean)).astype(BF16)
            if h % group == group - 1:
                parts += own_channels(keys_t, grad_score, h - group + 1)
        yield
        key_grads = dot(grad_score[...], query) * scale
        yield
        grad_query_t = jnp.concatenate(parts, axis=0) * scale
        grad_query = dot_nt(normed_t[...], grad_query_t.astype(BF16))
        yield grad_query, dot(table_t, key_grads.astype(BF16)), grad_value, grad_out

    running = [work(i) for i in range(count)]
    found = [None] * count
    while found[0] is None:
        found = [next(step) for step in running]
    crossed = reduce_groups(cells)[3]
    place = lax.axis_index("cell")
    core = place % 2
    for offset in crossed:
        core = core ^ ((place // offset) % 2)
    for matrix in range(4):
        total = sum(part[matrix] for part in found[1:]) + found[0][matrix]
        blocks = total.reshape((cells // 2, 2) + keep.shape[2:])
        for k in range(cells // 2):
            first = core == sum(2 * k // offset for offset in crossed) % 2
            keep[k, matrix] = jnp.where(first, blocks[k, 0], blocks[k, 1])
            send[k, matrix] = jnp.where(first, blocks[k, 1], blocks[k, 0]).astype(BF16)


def vmem(count):
    return [pl.BlockSpec(memory_space=pltpu.VMEM)] * count


SMEM = pl.BlockSpec(memory_space=pltpu.SMEM)


def struct(shape, dtype):
    return jax.ShapeDtypeStruct(shape, dtype)


def pinned(shape, dtype):
    return pltpu.VMEM(shape, dtype)


def halvings(size):
    offsets = []
    offset = size // 2
    while offset:
        offsets.append(offset)
        offset //= 2
    return offsets


def crossing(offset, crossed):
    return offset | 1 if offset in crossed else offset


def swap(array, cells, vector_of):
    return lax.ppermute(array, "cell", [(i, i ^ vector_of(i)) for i in range(cells)])


def gather_cells(shard, cells, beside):
    place = lax.axis_index("cell")
    offsets = halvings(cells)[:-1]
    far, (a, b) = offsets[:-2], offsets[-2:]
    crossed = [*far, a]
    held = shard
    done = ()

    def step(vectors):
        nonlocal done
        work = beside.pop(0)(*done) if beside else done
        arrived = [swap(held, cells, lambda i, vector=vector: vector) for vector in vectors]
        done, arrived = lax.optimization_barrier((work, arrived))
        return arrived

    def placed(first, second, offset):
        own = (place // offset) % 2 == 0
        return jnp.where(own, jnp.stack([first, second]), jnp.stack([second, first]))

    for offset in far:
        held = placed(held, step([crossing(offset, crossed)])[0], offset)
    vectors = [crossing(offset, crossed) for offset in (a, b)]
    over_both, over_a, over_b = step([vectors[0] ^ vectors[1], *vectors])
    held = placed(placed(held, over_b, b), placed(over_a, over_both, b), a)
    (arrived,) = step([1])
    return held, arrived, done


def assemble(held, arrived, weights, cells):
    offsets = halvings(cells)[:-1]
    far, (a, b) = offsets[:-2], offsets[-2:]
    crossed = [*far, a]
    place = lax.axis_index("cell")
    core = place % 2
    for offset in crossed:
        core = core ^ ((place // offset) % 2)
    matrices, rows, _ = held.shape[-3:]
    for k in range(cells // 2):
        at = tuple(2 * k // offset % 2 for offset in (a, b, *reversed(far)))
        first = core == sum(2 * k // offset for offset in crossed) % 2
        for matrix in range(matrices):
            own, other = held[(*at, matrix)], arrived[(*at, matrix)]
            pair = [jnp.where(first, own, other), jnp.where(first, other, own)]
            if rows % 16:
                pair = [part.astype(F32) for part in pair]
            weights[matrix, 2 * k * rows : 2 * (k + 1) * rows, :] = jnp.concatenate(pair, axis=0).astype(BF16)


def reduce_groups(cells):
    left = halvings(cells)[:-1]
    near, middle, farthest = left[-2:], left[1:-2], left[0]
    return near, middle, farthest, [near[0], *middle, farthest]


def reduce_all(keep, send, cells, bricks, across):
    place = lax.axis_index("cell")
    left = halvings(cells)[:-1]
    near, middle, farthest, crossed = reduce_groups(cells)
    total = keep + swap(send, cells, lambda i: 1).astype(F32)
    total = total.reshape((2,) * len(left) + keep.shape[1:])

    def portion(array, flipped):
        for offset, flip in reversed(flipped):
            bit = (place // offset) % 2
            array = lax.dynamic_index_in_dim(array, 1 - bit if flip else bit, left.index(offset), False)
        return array

    def exchange(group):
        nonlocal total, left
        mine = portion(total, [(offset, 0) for offset in group])
        for step in (2, 3, 1) if len(group) == 2 else (1,):
            flipped = [(offset, step >> k & 1) for k, offset in enumerate(group)]
            vector = 0
            for offset, flip in flipped:
                vector ^= crossing(offset, crossed) * flip
            sent = portion(total, flipped).astype(BF16)
            mine = mine + swap(sent, cells, lambda i, vector=vector: vector).astype(F32)
        total = mine
        left = [offset for offset in left if offset not in group]

    exchange(near)
    for offset in reversed(middle):
        exchange([offset])

    def meet(array, vector, step):
        pairs = [
            (cell * bricks + brick, (cell ^ vector) * bricks + (brick ^ step))
            for cell in range(cells)
            for brick in range(bricks)
        ]
        return lax.ppermute(array, ("cell", "brick"), pairs).astype(F32)

    vector = crossing(farthest, crossed)
    keep = portion(total, [(farthest, 0)])
    send = portion(total, [(farthest, 1)]).astype(BF16)
    if across:
        keep = keep.astype(BF16)
    total = keep.astype(F32) + meet(send, vector, 0)
    if across:
        far = meet(send, vector, across[0])
        total = total + (far + meet(keep, 0, across[0]))
    for step in across[1:]:
        keep = total.astype(BF16)
        total = keep.astype(F32) + meet(keep, 0, step)
    return total


def body(
    cells,
    bricks,
    features,
    species,
    species_table,
    neighbours,
    counts,
    send_lists,
    distances,
    head_decay,
    norm_gain,
    readout,
    targets,
    master,
    moment,
    second,
):
    atoms, width = features.shape[2:]
    slots = neighbours.shape[2]
    ghost_slots = send_lists.shape[3]
    heads = head_decay.shape[0]
    table_rows = atoms + bricks * ghost_slots

    paired = bricks == 2 and table_rows <= 256
    count = 2 if paired else 1
    brick = lax.axis_index("brick")
    part = table_rows // 2
    own = (features[0, 0], species[0], send_lists[0, 0])
    slot_arrays = (neighbours[0, 0], counts[0], distances[0, 0], targets[0])
    common = (species_table, norm_gain[None])
    embed_shapes = (
        pinned((atoms, width), F32),
        pinned((atoms, width), BF16),
        pinned((width, atoms), BF16),
        pinned((bricks, ghost_slots, width), BF16),
    )
    slot_shapes = tuple(pinned(array.shape, array.dtype) for array in slot_arrays)
    small = pltpu.CompilerParams(vmem_limit_bytes=8 * 1024 * 1024)

    def embed_own():
        rest = (head_decay[None], readout[None], *common)
        shapes = (pinned(master.shape, BF16),) + embed_shapes + slot_shapes
        shapes += tuple(pinned(array.shape, array.dtype) for array in rest)
        if paired:
            shapes += (pinned((width + 4 * slots + PACK_ROWS, atoms), BF16),)
        outs = pl.pallas_call(
            functools.partial(embed_kernel, int(paired)),
            out_shape=shapes,
            in_specs=vmem(6 + len(slot_arrays) + len(rest)),
            out_specs=tuple(vmem(len(shapes))),
            name="embed",
        )(master, *own, *common, *slot_arrays, *rest)
        return outs[0], outs[1:5], outs[5:9], outs[9:13], outs[13:]

    def embed_partner(packed, *common):
        outs = pl.pallas_call(
            unpack_kernel,
            out_shape=embed_shapes + slot_shapes,
            in_specs=vmem(3),
            out_specs=tuple(vmem(8)),
            compiler_params=small,
            name="unpack",
        )(packed, *common)
        return outs[:4], outs[4:]

    def index(first, arrays, decay):
        return pl.pallas_call(
            functools.partial(index_kernel, first),
            out_shape=(pinned((heads, part, atoms), F32), pinned((part, atoms), F32)),
            in_specs=vmem(4),
            out_specs=tuple(vmem(2)),
            scratch_shapes=[pltpu.VMEM((slots, atoms), jnp.int32)],
            compiler_params=small,
            name="index",
        )(*arrays[:3], decay)

    def over_bricks(array, offset):
        return lax.ppermute(array, "brick", [(i, i ^ offset) for i in range(bricks)])

    def ghosts_from(parcel):
        ghosts = parcel
        for offset in range(1, bricks):
            peer = brick ^ offset
            arrived = over_bricks(lax.dynamic_index_in_dim(parcel, peer, 0, True), offset)
            ghosts = lax.dynamic_update_slice_in_dim(ghosts, arrived, peer, 0)
        return ghosts.reshape(bricks * ghost_slots, width)

    def ghosts_of(parcels, place):
        chosen = [lax.dynamic_index_in_dim(parcel, place, 0, False) for parcel in parcels]
        ordered = jnp.where(brick == 0, jnp.stack(chosen), jnp.stack(chosen[::-1]))
        return ordered.reshape(bricks * ghost_slots, width)

    late = []

    shard, state, arrays, (decay, gain, *kept), packed = embed_own()

    def prepare():
        if paired:
            late.extend([over_bricks(packed[0], 1), *kept])
        return state, arrays, decay, gain, index(0, arrays, decay)

    def gather_ghosts(state, arrays, decay, gain, half):
        rows = ghosts_from(state[3])
        return [(state, rows, arrays[3], half, index(part, arrays, decay))], gain

    def visit_partner(state, arrays, decay, gain, half):
        rest = index(part, arrays, decay)
        partner, partner_arrays = embed_partner(*late)
        partner_half = index(0, partner_arrays, decay)
        return (state, arrays[3], half, rest), (partner, partner_arrays, partner_half), decay, gain

    def finish_partner(mine, other, decay, gain):
        state, wanted, half, rest = mine
        partner, arrays, partner_half = other
        parcels = (state[3], partner[3])
        return [
            (state, ghosts_of(parcels, brick), wanted, half, rest),
            (partner, ghosts_of(parcels, 1 - brick), arrays[3], partner_half, index(part, arrays, decay)),
        ], gain

    steps = [prepare, *[lambda *done: done] * (len(halvings(cells)) - 4)]
    steps += [visit_partner, finish_partner] if paired else [gather_ghosts]
    held, arrived, (worked, gain) = gather_cells(shard, cells, steps)
    operands = []
    for (embedded, normed, normed_t, _), ghosts, wanted, half, rest in worked:
        operands += [normed, normed_t, ghosts, embedded, *half, *rest, wanted]

    columns = heads * atoms
    blocks = (cells // 2,) + master.shape
    energies, keep, send = pl.pallas_call(
        functools.partial(sweep_kernel, count, cells),
        out_shape=(struct((1, atoms), F32), pinned(blocks, F32), pinned(blocks, BF16)),
        in_specs=vmem(3 + len(operands)),
        out_specs=tuple(vmem(3)),
        scratch_shapes=[
            pltpu.VMEM((table_rows, columns), F32),
            pltpu.VMEM((table_rows, columns), F32),
            pltpu.VMEM((table_rows, columns), BF16),
            pltpu.VMEM((table_rows, columns), BF16),
        ]
        * count
        + [pltpu.VMEM((master.shape[0], width, width), BF16)],
        compiler_params=pltpu.CompilerParams(vmem_limit_bytes=32 * 1024 * 1024),
        name="sweep",
    )(held, arrived, gain, *operands)

    across = [] if paired else list(reversed(halvings(bricks)))
    owned = reduce_all(keep, send, cells, bricks, across)
    moment_new = 0.9 * moment + 0.1 * owned
    second_new = 0.999 * second + 0.001 * owned * owned
    adam_step = moment_new / (jnp.sqrt(second_new) + 1e-08)
    return (energies[None], moment_new, second_new, adam_step)


def solution(mesh):
    return jax.shard_map(
        functools.partial(body, mesh.shape["cell"], mesh.shape["brick"]),
        mesh=mesh,
        in_specs=(
            P("cell", "brick", None, None),
            P("cell", "brick", None),
            P(),
            P("cell", "brick", None, None),
            P("cell", "brick", None),
            P("cell", "brick", None, None),
            P("cell", "brick", None, None),
            P(),
            P(),
            P(),
            P("cell", "brick", None),
            P(None, "cell", None),
            P(None, "cell", None),
            P(None, "cell", None),
        ),
        out_specs=(
            P("cell", "brick", None),
            P(None, "cell", None),
            P(None, "cell", None),
            P(None, "cell", None),
        ),
        check_vma=False,
    )
```
